256 devices in a mesh: row: 16 (over x_hi, z), col: 16 (over x_lo, y, core).
Axes of the slice: x: 4 (x_hi: 2, x_lo: 2; x = x_hi * 2 + x_lo), y: 4, z: 8, core: 2. Of those that a mesh axis runs over, the one named last changes fastest.
Arguments:
- target_state: float32 [12, 32768], P(None, ('row', 'col')), may hold values from -6 to 6
- target_mass: float32 [32768], P(('row', 'col')), may hold values from 0.25 to 4
- source_state: float32 [12, 32768], P(None, ('row', 'col')), may hold values from -6 to 6
- source_mass: float32 [32768], P(('row', 'col')), may hold values from 0.25 to 4
Outputs:
- target_next: float32 [12, 32768], P(None, ('row', 'col'))
- source_pull: float32 [6, 32768], P(None, ('row', 'col'))
The draws below stay inside these ranges and needn't reach their ends.
All inputs are finite; a program needn't handle non-finite values.
Results may differ from the reference program's by a relative error of at most 0.0003.
Values sent between devices are 32-bit elements; how exact they have to be, the bound alone decides.
A program may use at most 64 MiB of HBM per device.

```python
import math
import jax
import jax.numpy as jnp
from jax import lax

TARGETS = 32768
SOURCES = 32768


def block_scale(stream_key, shape, shards, least, top_value):
    gain = 1.0
    for dim, blocks in shards:
        heights = jax.random.uniform(jax.random.fold_in(jax.random.fold_in(stream_key, 6), dim), (blocks,), jnp.float32, least / len(shards), top_value / len(shards))
        gain = gain * jnp.repeat(jnp.exp(heights), shape[dim] // blocks).reshape((-1,) + (1,) * (len(shape) - 1 - dim))
    return gain


def noise(rng, shape, deviation, bound, split=(), kind=jnp.bfloat16):
    entries = jax.random.normal(rng, shape, jnp.float32) * deviation
    if len(split) > 0:
        entries = block_scale(rng, shape, split, -0.22, 0.18) * entries
    return jnp.clip(entries, min=-bound, max=bound).astype(kind)


def setup_inputs(seed: int = 0) -> dict:
    streams_of = jax.random.split(jax.random.key(seed), 5)
    return {
        "target_state": noise(streams_of[0], (12, TARGETS), 1.0, 6.0, ((1, 256),), jnp.float32),
        "target_mass": jnp.clip(jnp.exp(math.log(4.0) - 2.7725887 * jax.random.uniform(streams_of[1], (TARGETS,), jnp.float32) ** block_scale(streams_of[1], (TARGETS,), ((0, 256),), -0.2, 0.2)), 0.25, 4.0),
        "source_state": noise(streams_of[2], (12, SOURCES), 1.0, 6.0, ((1, 256),), jnp.float32),
        "source_mass": jnp.clip(jnp.exp(math.log(4.0) - 2.7725887 * jax.random.uniform(streams_of[3], (SOURCES,), jnp.float32) ** block_scale(streams_of[3], (SOURCES,), ((0, 256),), -0.2, 0.2)), 0.25, 4.0),
    }


STEP = 0.25
SOFTEN = 0.0025

def predict(state):
    position = state[0:3]
    velocity = state[3:6]
    accel = state[6:9]
    jerks = state[9:12]
    new_position = position + STEP * (velocity + STEP * (0.5 * accel + STEP / 6.0 * jerks))
    new_velocity = velocity + STEP * (accel + 0.5 * STEP * jerks)
    return jnp.concatenate([new_position, new_velocity], axis=0)

def interact(targets, target_weight, sources, source_weight):
    offset = sources[0:3, None, :] - targets[0:3, :, None]
    relative = sources[3:6, None, :] - targets[3:6, :, None]
    square = lax.optimization_barrier(jnp.sum(offset * offset, axis=0)) + SOFTEN
    inverse = lax.rsqrt(square)
    inverse_two = inverse * inverse
    inverse_three = inverse * inverse_two
    radial = 3.0 * lax.optimization_barrier(jnp.sum(offset * relative, axis=0)) * inverse_two
    change = relative - radial[None] * offset
    on_target = inverse_three * source_weight[None, :]
    on_source = inverse_three * target_weight[:, None]
    target_terms = jnp.concatenate([lax.optimization_barrier(jnp.sum(offset * on_target[None], axis=2)), lax.optimization_barrier(jnp.sum(change * on_target[None], axis=2))], axis=0)
    source_terms = -jnp.concatenate([lax.optimization_barrier(jnp.sum(offset * on_source[None], axis=1)), lax.optimization_barrier(jnp.sum(change * on_source[None], axis=1))], axis=0)
    return (target_terms, source_terms)

def correct(state, totals):
    position = state[0:3]
    velocity = state[3:6]
    accel = state[6:9]
    jerks = state[9:12]
    new_accel = totals[0:3]
    new_jerks = totals[3:6]
    new_velocity = velocity + 0.5 * STEP * (accel + new_accel) + STEP * STEP / 12.0 * (jerks - new_jerks)
    new_position = position + 0.5 * STEP * (velocity + new_velocity) + STEP * STEP / 12.0 * (accel - new_accel)
    return jnp.concatenate([new_position, new_velocity, new_accel, new_jerks], axis=0)

def reference(target_state, target_mass, source_state, source_mass):
    targets = predict(target_state)
    target_weight = target_mass / TARGETS
    sources = predict(source_state)
    source_weight = source_mass / SOURCES
    width = min(256, SOURCES)
    count = SOURCES // width
    blocks = sources.reshape(6, count, width).transpose(1, 0, 2)
    weights = source_weight.reshape(count, width)

    def advance(total, item):
        block, weight = item
        target_terms, source_terms = interact(targets, target_weight, block, weight)
        return (total + target_terms, source_terms)
    totals, pulls = lax.scan(advance, jnp.zeros((6, TARGETS), jnp.float32), (blocks, weights))
    source_pull = pulls.transpose(1, 0, 2).reshape(6, SOURCES)
    return (correct(target_state, totals), source_pull)
```

```python
import functools

import jax
import jax.numpy as jnp
from jax import lax
from jax.experimental import pallas as pl
from jax.experimental.pallas import tpu as pltpu
from jax.sharding import PartitionSpec as P

STEP = 0.25
SOFTEN = 0.0025
MESH = pl.DeviceIdType.MESH
f32, bf16 = jnp.float32, jnp.bfloat16
OWN = 128


def dot(a, b, ca, cb):
    return lax.dot_general(a, b, (((ca,), (cb,)), ((), ())), preferred_element_type=f32)


def pieces(x):
    high = x.astype(bf16).astype(f32)
    rest = x - high
    mid = rest.astype(bf16).astype(f32)
    return high, mid, (rest - mid).astype(bf16).astype(f32)


def halves(x):
    high = x.astype(bf16)
    return high, (x - high.astype(f32)).astype(bf16)


def predict(state, mass):
    x, v, a, j = state[0:3], state[3:6], state[6:9], state[9:12]
    xp = x + STEP * (v + STEP * (0.5 * a + STEP / 6.0 * j))
    vp = v + STEP * (a + 0.5 * STEP * j)
    return jnp.concatenate([xp, vp, jnp.ones_like(mass), mass], axis=0)


def moments(tile):
    row = lax.broadcasted_iota(jnp.int32, tile.shape, 0)
    mass = jnp.broadcast_to(tile[7:8], tile.shape)
    first = jnp.where(row < 7, tile * mass, 0.0)
    moved = pltpu.roll(first, 3, 0)
    second = jnp.where(row == 7, mass, jnp.where((row >= 3) & (row < 6), -moved, 0.0))
    zero = jnp.zeros_like(tile)
    return (
        jnp.concatenate([*pieces(first), zero], axis=0).astype(bf16),
        jnp.concatenate([*pieces(second), zero], axis=0).astype(bf16),
    )


def resolve(total, tile):
    x, v = tile[0:3], tile[3:6]
    accel = total[0:3] - x * total[6:7]
    jerk = total[3:6] - v * total[6:7] + x * total[7:8]
    return accel, jerk


def kernel(rows, cols, ts_ref, tm_ref, ss_ref, sm_ref, next_ref, pull_ref,
           tgat, sgat, ft, fs, rc, rg, tc, tg, xb, xs, osum, tsum, pt, ps, qt, qs, send, recv):
    row, col = lax.axis_index("row"), lax.axis_index("col")
    BI, BK = 256, 512
    nt, ns = cols * OWN, rows * OWN

    def in_col(e):
        return (row, lax.rem(col + e, cols))

    def in_row(e):
        return (lax.rem(row + e, rows), col)

    barrier = pltpu.get_barrier_semaphore()
    for e in range(1, cols):
        pl.semaphore_signal(barrier, inc=1, device_id=in_col(e), device_id_type=MESH)
    for e in range(1, rows):
        pl.semaphore_signal(barrier, inc=1, device_id=in_row(e), device_id_type=MESH)

    tgat[cols - 1] = predict(ts_ref[...], tm_ref[...] * (1.0 / (nt * rows)))
    sgat[rows - 1] = predict(ss_ref[...], sm_ref[...] * (1.0 / (ns * cols)))
    osum[...] = jnp.zeros_like(osum)
    tsum[...] = jnp.zeros_like(tsum)
    pl.semaphore_wait(barrier, cols + rows - 2)

    def t_gather(e):
        return pltpu.make_async_remote_copy(
            src_ref=tgat.at[cols - 1], dst_ref=tgat.at[cols - 1 - e], send_sem=send.at[0, e],
            recv_sem=recv.at[0, cols - 1 - e], device_id=in_col(e), device_id_type=MESH)

    def s_gather(e):
        return pltpu.make_async_remote_copy(
            src_ref=sgat.at[rows - 1], dst_ref=sgat.at[rows - 1 - e], send_sem=send.at[1, e],
            recv_sem=recv.at[1, rows - 1 - e], device_id=in_row(e), device_id_type=MESH)

    def t_return(d):
        return pltpu.make_async_remote_copy(
            src_ref=pt.at[d], dst_ref=qt.at[cols - 2 - d], send_sem=send.at[2, d],
            recv_sem=recv.at[2, cols - 2 - d], device_id=in_col(d + 1), device_id_type=MESH)

    def s_return(d):
        return pltpu.make_async_remote_copy(
            src_ref=ps.at[d], dst_ref=qs.at[rows - 2 - d], send_sem=send.at[3, d],
            recv_sem=recv.at[3, rows - 2 - d], device_id=in_row(d + 1), device_id_type=MESH)

    for e in range(1, rows):
        s_gather(e).start()
    for e in range(1, cols):
        t_gather(e).start()

    zeros = jnp.zeros((OWN - 48, OWN), f32)

    def prepare_source(d):
        tile = sgat[d]
        at = pl.ds(pl.multiple_of(d * OWN, OWN), OWN)
        rc[:, at], rg[:, at] = moments(tile)
        x, v = tile[0:3], tile[3:6]
        vec = jnp.concatenate([-3.0 * v, -3.0 * x, 3.0 * jnp.sum(x * v, axis=0, keepdims=True), tile[6:7]], axis=0)
        h, m, l = pieces(vec)
        fs[:, at] = jnp.concatenate([h, m, h, m, l, h, zeros], axis=0).astype(bf16)
        xs[:, at] = tile

    def prepare_target(d):
        tile = tgat[d]
        at = pl.ds(pl.multiple_of(d * OWN, OWN), OWN)
        tc[:, at], tg[:, at] = moments(tile)
        x, v = tile[0:3], tile[3:6]
        vec = jnp.concatenate([x, v, tile[6:7], 3.0 * jnp.sum(x * v, axis=0, keepdims=True)], axis=0)
        h, m, l = pieces(vec)
        ft[at, :] = jnp.concatenate([h, h, m, m, h, l, zeros], axis=0).T.astype(bf16)
        for c in range(3):
            xb[at, c * OWN:(c + 1) * OWN] = jnp.broadcast_to(tile[c:c + 1], (OWN, OWN)).T

    def arrive_source(d, _):
        @pl.when(d < rows - 1)
        def _():
            s_gather(rows - 1 - d).wait_recv()
        prepare_source(d)
        return 0

    def arrive_target(d, _):
        @pl.when(d < cols - 1)
        def _():
            t_gather(cols - 1 - d).wait_recv()
        prepare_target(d)
        return 0

    lax.fori_loop(0, rows, arrive_source, 0)
    lax.fori_loop(0, cols, arrive_target, 0)

    def tile(i0, k0):
        i, k = pl.ds(i0, BI), pl.ds(k0, BK)
        dw = dot(ft[i, :], fs[:, k], 1, 0)
        s = SOFTEN
        for c in range(3):
            left = xb[i, c * OWN:(c + 1) * OWN]
            d = xs[c:c + 1, k] - jnp.concatenate([left] * (BK // OWN), axis=1)
            s = d * d + s
        q = lax.rsqrt(s)
        q2 = q * q
        c = q * q2
        g = (dw * q2) * c
        ch, cl = halves(c)
        gh, gl = halves(g)
        tci, tgi, rck, rgk = tc[:, i], tg[:, i], rc[:, k], rg[:, k]
        osum[:, k] += dot(jnp.concatenate([tci, tci, tgi, tgi], axis=1),
                          jnp.concatenate([ch, cl, gh, gl], axis=0), 1, 0)
        tsum[:, i] += dot(jnp.concatenate([rck, rck, rgk, rgk], axis=1),
                          jnp.concatenate([ch, cl, gh, gl], axis=1), 1, 1)

    def fold(total):
        return total[0:8] + total[8:16] + total[16:24]

    def strip(n, _):
        i0 = pl.multiple_of(n * BI, BI)

        def part(p, _):
            for u in range(2):
                tile(i0, pl.multiple_of((p * 2 + u) * BK, BK))
            return 0

        lax.fori_loop(0, ns // (2 * BK), part, 0)
        for u in range(BI // OWN):
            d = n * (BI // OWN) + u
            pt[d] = fold(tsum[:, pl.ds(pl.multiple_of(d * OWN, OWN), OWN)])

            @pl.when(d < cols - 1)
            def _():
                t_return(d).start()
        return 0

    lax.fori_loop(0, nt // BI, strip, 0)
    for d in range(rows):
        ps[d] = fold(osum[:, d * OWN:(d + 1) * OWN])
        if d < rows - 1:
            s_return(d).start()

    def settle_target(d, total):
        t_return(cols - 2 - d).wait_recv()
        return total + qt[d]

    total = lax.fori_loop(0, cols - 1, settle_target, pt[cols - 1])
    a1, j1 = resolve(total, tgat[cols - 1])
    x, v, a, j = ts_ref[0:3], ts_ref[3:6], ts_ref[6:9], ts_ref[9:12]
    v1 = v + 0.5 * STEP * (a + a1) + STEP * STEP / 12.0 * (j - j1)
    x1 = x + 0.5 * STEP * (v + v1) + STEP * STEP / 12.0 * (a - a1)
    next_ref[...] = jnp.concatenate([x1, v1, a1, j1], axis=0)

    def settle_source(d, total):
        s_return(rows - 2 - d).wait_recv()
        return total + qs[d]

    total = lax.fori_loop(0, rows - 1, settle_source, ps[rows - 1])
    pull_ref[...] = jnp.concatenate(resolve(total, sgat[rows - 1]), axis=0)

    for e in range(1, rows):
        s_gather(e).wait_send()
        s_return(e - 1).wait_send()
    for e in range(1, cols):
        t_gather(e).wait_send()
        t_return(e - 1).wait_send()


def solution(mesh):
    rows, cols = mesh.shape["row"], mesh.shape["col"]
    nt, ns = cols * OWN, rows * OWN
    vmem = pl.BlockSpec(memory_space=pltpu.VMEM)
    call = pl.pallas_call(
        functools.partial(kernel, rows, cols),
        out_shape=(jax.ShapeDtypeStruct((12, OWN), f32), jax.ShapeDtypeStruct((6, OWN), f32)),
        in_specs=[vmem] * 4,
        out_specs=(vmem, vmem),
        scratch_shapes=[
            pltpu.VMEM((cols, 8, OWN), f32),
            pltpu.VMEM((rows, 8, OWN), f32),
            pltpu.VMEM((nt, OWN), bf16),
            pltpu.VMEM((OWN, ns), bf16),
            pltpu.VMEM((32, ns), bf16),
            pltpu.VMEM((32, ns), bf16),
            pltpu.VMEM((32, nt), bf16),
            pltpu.VMEM((32, nt), bf16),
            pltpu.VMEM((nt, 3 * OWN), f32),
            pltpu.VMEM((8, ns), f32),
            pltpu.VMEM((32, ns), f32),
            pltpu.VMEM((32, nt), f32),
            pltpu.VMEM((cols, 8, OWN), f32),
            pltpu.VMEM((rows, 8, OWN), f32),
            pltpu.VMEM((cols, 8, OWN), f32),
            pltpu.VMEM((rows, 8, OWN), f32),
            pltpu.SemaphoreType.DMA((4, 16)),
            pltpu.SemaphoreType.DMA((4, 16)),
        ],
        compiler_params=pltpu.CompilerParams(
            collective_id=0, has_side_effects=True, vmem_limit_bytes=48 << 20),
    )

    def shards(target_state, target_mass, source_state, source_mass):
        return call(target_state, target_mass.reshape(1, OWN), source_state, source_mass.reshape(1, OWN))

    spec = P(None, ("row", "col"))
    line = P(("row", "col"))
    return jax.shard_map(shards, mesh=mesh, in_specs=(spec, line, spec, line),
                         out_specs=(spec, spec), check_vma=False)
```

```python
import jax
import jax.numpy as jnp
import numpy as np
from jax import lax
from jax.experimental import pallas as pl
from jax.experimental.pallas import tpu as pltpu
from jax.sharding import PartitionSpec as P

STEP = 0.25
SOFTEN = 0.0025
MESH = pl.DeviceIdType.MESH
f32, bf16 = jnp.float32, jnp.bfloat16
OWN = 128


def dot(a, b, ca, cb):
    return lax.dot_general(a, b, (((ca,), (cb,)), ((), ())), preferred_element_type=f32)


def pieces(x):
    high = x.astype(bf16).astype(f32)
    rest = x - high
    mid = rest.astype(bf16).astype(f32)
    return high, mid, (rest - mid).astype(bf16).astype(f32)


def halves(x):
    high = x.astype(bf16)
    return high, (x - high.astype(f32)).astype(bf16)


def predict(state, mass):
    x, v, a, j = state[0:3], state[3:6], state[6:9], state[9:12]
    xp = x + STEP * (v + STEP * (0.5 * a + STEP / 6.0 * j))
    vp = v + STEP * (a + 0.5 * STEP * j)
    return jnp.concatenate([xp, vp, jnp.ones_like(mass), mass], axis=0)


def moments(tile):
    row = lax.broadcasted_iota(jnp.int32, tile.shape, 0)
    mass = jnp.broadcast_to(tile[7:8], tile.shape)
    first = jnp.where(row < 7, tile * mass, 0.0)
    moved = pltpu.roll(first, 3, 0)
    second = jnp.where(row == 7, mass, jnp.where((row >= 3) & (row < 6), -moved, 0.0))
    zero = jnp.zeros_like(tile)
    return (
        jnp.concatenate([*pieces(first), zero], axis=0).astype(bf16),
        jnp.concatenate([*pieces(second), zero], axis=0).astype(bf16),
    )


def resolve(total, tile):
    x, v = tile[0:3], tile[3:6]
    accel = total[0:3] - x * total[6:7]
    jerk = total[3:6] - v * total[6:7] + x * total[7:8]
    return accel, jerk


def order(offsets, distance, groups):
    left = sorted((o for o in offsets if any(o)), key=distance)
    return groups(left) + [o for o in offsets if not any(o)]


ROW_SIZES, COL_SIZES = (2, 8), (2, 4, 2)


def offsets(sizes):
    return list(np.ndindex(*sizes))


def row_hops(o):
    return 2 * o[0] + min(o[1], 8 - o[1])


def col_hops(o):
    return o[0] + min(o[1], 4 - o[1]) + 0.5 * o[2]


def spread(near):
    return near[:4] + near[4:][::-1]


ROW_SLOTS = order(offsets(ROW_SIZES), row_hops, spread)
COL_SLOTS = order(offsets(COL_SIZES), col_hops, list)


def inverse(slots, sizes):
    return [slots.index(tuple(-a % n for a, n in zip(o, sizes))) for o in slots]


ROW_BACK, COL_BACK = inverse(ROW_SLOTS, ROW_SIZES), inverse(COL_SLOTS, COL_SIZES)
LAST = 15
BI = BK = 256


def moved(index, offset, sizes):
    out, unit = 0, 1
    for o, n in reversed(list(zip(offset, sizes))):
        out = out + lax.rem(lax.div(index, unit) + o, n) * unit
        unit *= n
    return out


def kernel(ts_hbm, tm_hbm, ss_hbm, sm_hbm, next_ref, pull_ref, ts_ref, tm_ref, ss_ref, sm_ref,
           tgat, sgat, ft, fs, rc, rg, tc, tg, xb, xs, tsum, pt, ps, qt, qs, pair, turned, send, recv, load):
    row, col = lax.axis_index("row"), lax.axis_index("col")
    row_peer = [(moved(row, o, ROW_SIZES), col) for o in ROW_SLOTS]
    col_peer = [(row, moved(col, o, COL_SIZES)) for o in COL_SLOTS]
    far = sorted([(-row_hops(ROW_SLOTS[p]), 0, p) for p in range(LAST)]
                 + [(-col_hops(COL_SLOTS[p]), 1, p) for p in range(LAST)])

    barrier = pltpu.get_barrier_semaphore()
    for _, axis, p in far:
        pl.semaphore_signal(barrier, inc=1, device_id=(row_peer, col_peer)[axis][p], device_id_type=MESH)
    loads = [pltpu.make_async_copy(a, b, load.at[n]) for n, (a, b) in enumerate(
        ((ts_hbm, ts_ref), (tm_hbm, tm_ref), (ss_hbm, ss_ref), (sm_hbm, sm_ref)))]
    for copy in loads:
        copy.start()
    tsum[...] = jnp.zeros_like(tsum)
    for copy in loads:
        copy.wait()
    tgat[LAST] = predict(ts_ref[...], tm_ref[...] * (1.0 / 32768))
    sgat[LAST] = predict(ss_ref[...], sm_ref[...] * (1.0 / 32768))
    pl.semaphore_wait(barrier, 2 * LAST)

    def copy_to(src, dst, kind, p, back, peer):
        return pltpu.make_async_remote_copy(
            src_ref=src, dst_ref=dst.at[back[p]], send_sem=send.at[kind, p],
            recv_sem=recv.at[kind, back[p]], device_id=peer[p], device_id_type=MESH)

    def arrived(src, dst, kind, p, peer):
        pltpu.make_async_remote_copy(
            src_ref=src, dst_ref=dst.at[p], send_sem=send.at[kind, 0],
            recv_sem=recv.at[kind, p], device_id=peer[0], device_id_type=MESH).wait_recv()

    gathers = [(copy_to(sgat.at[LAST], sgat, 0, p, ROW_BACK, row_peer),
                copy_to(tgat.at[LAST], tgat, 1, p, COL_BACK, col_peer))[axis] for _, axis, p in far]
    for copy in gathers:
        copy.start()
    source_returns = [copy_to(ps.at[p], qs, 2, p, ROW_BACK, row_peer) for p in range(LAST)]
    target_returns = [copy_to(pt.at[p], qt, 3, p, COL_BACK, col_peer) for p in range(LAST)]

    zeros = jnp.zeros((OWN - 48, OWN), f32)

    def prepare_source(d):
        tile = sgat[d]
        at = pl.ds(pl.multiple_of(d * OWN, OWN), OWN)
        rc[:, at], rg[:, at] = moments(tile)
        x, v = tile[0:3], tile[3:6]
        vec = jnp.concatenate([-3.0 * v, -3.0 * x, 3.0 * jnp.sum(x * v, axis=0, keepdims=True), tile[6:7]], axis=0)
        h, m, l = pieces(vec)
        fs[:, at] = jnp.concatenate([h, m, h, m, l, h, zeros], axis=0).astype(bf16)
        xs[:, at] = tile

    def prepare_target(d):
        tile = tgat[d]
        at = pl.ds(pl.multiple_of(d * OWN, OWN), OWN)
        tc[:, at], tg[:, at] = moments(tile)
        x, v = tile[0:3], tile[3:6]
        vec = jnp.concatenate([x, v, tile[6:7], 3.0 * jnp.sum(x * v, axis=0, keepdims=True)], axis=0)
        h, m, l = pieces(vec)
        ft[at, :] = jnp.concatenate([h, h, m, m, h, l, zeros], axis=0).T.astype(bf16)
        for c in range(3):
            xb[at, c * OWN:(c + 1) * OWN] = jnp.broadcast_to(tile[c:c + 1], (OWN, OWN)).T

    def arrive_targets(n, _):
        for u in range(4):
            @pl.when(n * 4 + u < LAST)
            def _():
                arrived(tgat.at[LAST], tgat, 1, n * 4 + u, col_peer)
        for u in range(4):
            prepare_target(n * 4 + u)
        return 0

    lax.fori_loop(0, 4, arrive_targets, 0)

    def fold(total):
        return total[0:8] + total[8:16] + total[16:24]

    tiles = tsum.shape[1] // BI

    def strip(n, _):
        for u in range(BK // OWN):
            p = n * (BK // OWN) + u

            @pl.when(p < LAST)
            def _():
                arrived(sgat.at[LAST], sgat, 0, p, row_peer)
        for u in range(BK // OWN):
            prepare_source(n * (BK // OWN) + u)
        k = pl.ds(pl.multiple_of(n * BK, BK), BK)
        rck, rgk, fsk = rc[:, k], rg[:, k], fs[:, k]
        r4 = jnp.concatenate([rck, rck, rgk, rgk], axis=1)
        pulls = jnp.zeros((32, BK), f32)
        for t in range(tiles + 1):
            if t < tiles:
                i = slice(t * BI, (t + 1) * BI)
                dw = dot(ft[i, :], fsk, 1, 0)
                s = SOFTEN
                for c in range(3):
                    left = xb[i, c * OWN:(c + 1) * OWN]
                    d = xs[c:c + 1, k] - jnp.concatenate([left] * (BK // OWN), axis=1)
                    s = d * d + s
                q = lax.rsqrt(s)
                q2 = q * q
                c = q * q2
                g = (dw * q2) * c
                for x, part in enumerate(halves(c) + halves(g)):
                    pair[t % 2, x] = part
                for x in range(4):
                    turned[t % 2, x] = pair[t % 2, x].T
            if t > 0:
                i = slice((t - 1) * BI, t * BI)
                tci, tgi = tc[:, i], tg[:, i]
                here = [pair[(t - 1) % 2, x] for x in range(4)]
                across = [turned[(t - 1) % 2, x] for x in range(4)]
                pulls = pulls + dot(jnp.concatenate([tci, tci, tgi, tgi], axis=1),
                                    jnp.concatenate(here, axis=0), 1, 0)
                tsum[:, i] += dot(r4, jnp.concatenate(across, axis=0), 1, 0)
        pulls = fold(pulls)
        for u in range(BK // OWN):
            ps[n * (BK // OWN) + u] = pulls[:, u * OWN:(u + 1) * OWN]
        for m in range(LAST // 2 + 1):
            @pl.when(n == m)
            def _():
                for copy in source_returns[2 * m:2 * m + 2]:
                    copy.start()
        return 0

    lax.fori_loop(0, xs.shape[1] // BK, strip, 0)
    for p in sorted(range(LAST + 1), key=lambda p: -col_hops(COL_SLOTS[p])):
        pt[p] = fold(tsum[:, p * OWN:(p + 1) * OWN])
        if p < LAST:
            target_returns[p].start()
    for copy in gathers + source_returns:
        copy.wait_send()

    for p in range(LAST):
        arrived(ps.at[0], qs, 2, p, row_peer)
    pull_ref[...] = jnp.concatenate(resolve(sum((qs[p] for p in range(LAST)), ps[LAST]), sgat[LAST]), axis=0)

    for copy in target_returns:
        copy.wait_send()
    for p in range(LAST):
        arrived(pt.at[0], qt, 3, p, col_peer)
    a1, j1 = resolve(sum((qt[p] for p in range(LAST)), pt[LAST]), tgat[LAST])
    x, v, a, j = ts_ref[0:3], ts_ref[3:6], ts_ref[6:9], ts_ref[9:12]
    v1 = v + 0.5 * STEP * (a + a1) + STEP * STEP / 12.0 * (j - j1)
    x1 = x + 0.5 * STEP * (v + v1) + STEP * STEP / 12.0 * (a - a1)
    next_ref[...] = jnp.concatenate([x1, v1, a1, j1], axis=0)


def solution(mesh):
    n = (LAST + 1) * OWN
    vmem, hbm = pl.BlockSpec(memory_space=pltpu.VMEM), pl.BlockSpec(memory_space=pl.ANY)
    slots = pltpu.VMEM((LAST + 1, 8, OWN), f32)
    call = pl.pallas_call(
        kernel,
        out_shape=(jax.ShapeDtypeStruct((12, OWN), f32), jax.ShapeDtypeStruct((6, OWN), f32)),
        in_specs=[hbm] * 4,
        out_specs=(vmem, vmem),
        scratch_shapes=[
            pltpu.VMEM((12, OWN), f32),
            pltpu.VMEM((1, OWN), f32),
            pltpu.VMEM((12, OWN), f32),
            pltpu.VMEM((1, OWN), f32),
            slots,
            slots,
            pltpu.VMEM((n, OWN), bf16),
            pltpu.VMEM((OWN, n), bf16),
            *[pltpu.VMEM((32, n), bf16)] * 4,
            pltpu.VMEM((n, 3 * OWN), f32),
            pltpu.VMEM((8, n), f32),
            pltpu.VMEM((32, n), f32),
            *[slots] * 4,
            pltpu.VMEM((2, 4, BI, BK), bf16),
            pltpu.VMEM((2, 4, BK, BI), bf16),
            pltpu.SemaphoreType.DMA((4, LAST)),
            pltpu.SemaphoreType.DMA((4, LAST)),
            pltpu.SemaphoreType.DMA((4,)),
        ],
        compiler_params=pltpu.CompilerParams(
            collective_id=0, has_side_effects=True, vmem_limit_bytes=48 << 20),
    )

    def shards(target_state, target_mass, source_state, source_mass):
        return call(target_state, target_mass.reshape(1, OWN), source_state, source_mass.reshape(1, OWN))

    spec = P(None, ("row", "col"))
    line = P(("row", "col"))
    return jax.shard_map(shards, mesh=mesh, in_specs=(spec, line, spec, line),
                         out_specs=(spec, spec), check_vma=False)
```

```python
import jax
import jax.numpy as jnp
import numpy as np
from jax import lax
from jax.experimental import pallas as pl
from jax.experimental.pallas import tpu as pltpu
from jax.sharding import PartitionSpec as P

STEP = 0.25
SOFTEN = 0.0025
MESH = pl.DeviceIdType.MESH
f32, bf16 = jnp.float32, jnp.bfloat16
OWN = 128


def dot(a, b, ca, cb):
    return lax.dot_general(a, b, (((ca,), (cb,)), ((), ())), preferred_element_type=f32)


def pieces(x):
    high = x.astype(bf16).astype(f32)
    rest = x - high
    mid = rest.astype(bf16).astype(f32)
    return high, mid, (rest - mid).astype(bf16).astype(f32)


def halves(x):
    high = x.astype(bf16)
    return high, (x - high.astype(f32)).astype(bf16)


def predict(state, mass):
    x, v, a, j = state[0:3], state[3:6], state[6:9], state[9:12]
    xp = x + STEP * (v + STEP * (0.5 * a + STEP / 6.0 * j))
    vp = v + STEP * (a + 0.5 * STEP * j)
    return jnp.concatenate([xp, vp, jnp.ones_like(mass), mass], axis=0)


def moments(tile):
    row = lax.broadcasted_iota(jnp.int32, tile.shape, 0)
    mass = jnp.broadcast_to(tile[7:8], tile.shape)
    first = jnp.where(row < 7, tile * mass, 0.0)
    moved = pltpu.roll(first, 3, 0)
    second = jnp.where(row == 7, mass, jnp.where((row >= 3) & (row < 6), -moved, 0.0))
    zero = jnp.zeros_like(tile)
    return (
        jnp.concatenate([*pieces(first), zero], axis=0).astype(bf16),
        jnp.concatenate([*pieces(second), zero], axis=0).astype(bf16),
    )


def resolve(total, tile):
    x, v = tile[0:3], tile[3:6]
    accel = total[0:3] - x * total[6:7]
    jerk = total[3:6] - v * total[6:7] + x * total[7:8]
    return accel, jerk


def order(offsets, distance, groups):
    left = sorted((o for o in offsets if any(o)), key=distance)
    return groups(left) + [o for o in offsets if not any(o)]


ROW_SIZES, COL_SIZES = (2, 8), (2, 4, 2)


def offsets(sizes):
    return list(np.ndindex(*sizes))


def row_hops(o):
    return 2 * o[0] + min(o[1], 8 - o[1])


def col_hops(o):
    return o[0] + min(o[1], 4 - o[1]) + 0.5 * o[2]


def spread(near):
    return near[:4] + near[4:][::-1]


ROW_SLOTS = order(offsets(ROW_SIZES), row_hops, spread)
COL_SLOTS = order(offsets(COL_SIZES), col_hops, list)


def inverse(slots, sizes):
    return [slots.index(tuple(-a % n for a, n in zip(o, sizes))) for o in slots]


ROW_BACK, COL_BACK = inverse(ROW_SLOTS, ROW_SIZES), inverse(COL_SLOTS, COL_SIZES)
LAST = 15
BI = BK = 256
WIDE = 2
SLOTS = WIDE * BK // OWN


def moved(index, offset, sizes):
    out, unit = 0, 1
    for o, n in reversed(list(zip(offset, sizes))):
        out = out + lax.rem(lax.div(index, unit) + o, n) * unit
        unit *= n
    return out


def kernel(ts_hbm, tm_hbm, ss_hbm, sm_hbm, next_ref, pull_ref, ts_ref, tm_ref, ss_ref, sm_ref,
           tgat, sgat, ft, fs, rc, rg, tc, tg, xb, xs, tsum, pt, ps, qt, qs, pair, turned, send, recv, load):
    row, col = lax.axis_index("row"), lax.axis_index("col")
    row_peer = [(moved(row, o, ROW_SIZES), col) for o in ROW_SLOTS]
    col_peer = [(row, moved(col, o, COL_SIZES)) for o in COL_SLOTS]
    far = sorted([(-row_hops(ROW_SLOTS[p]), 0, p) for p in range(LAST)]
                 + [(-col_hops(COL_SLOTS[p]), 1, p) for p in range(LAST)])

    loads = [pltpu.make_async_copy(a, b, load.at[n]) for n, (a, b) in enumerate(
        ((ts_hbm, ts_ref), (tm_hbm, tm_ref), (ss_hbm, ss_ref), (sm_hbm, sm_ref)))]
    for copy in loads:
        copy.start()
    barrier = pltpu.get_barrier_semaphore()
    for _, axis, p in far:
        pl.semaphore_signal(barrier, inc=1, device_id=(row_peer, col_peer)[axis][p], device_id_type=MESH)
    tsum[...] = jnp.zeros_like(tsum)
    for copy in loads:
        copy.wait()
    tgat[LAST] = predict(ts_ref[...], tm_ref[...] * (1.0 / 32768))
    sgat[LAST] = predict(ss_ref[...], sm_ref[...] * (1.0 / 32768))
    pl.semaphore_wait(barrier, 2 * LAST)

    def copy_to(src, dst, kind, p, back, peer):
        return pltpu.make_async_remote_copy(
            src_ref=src, dst_ref=dst.at[back[p]], send_sem=send.at[kind, p],
            recv_sem=recv.at[kind, back[p]], device_id=peer[p], device_id_type=MESH)

    def arrived(src, dst, kind, p, peer):
        pltpu.make_async_remote_copy(
            src_ref=src, dst_ref=dst.at[p], send_sem=send.at[kind, 0],
            recv_sem=recv.at[kind, p], device_id=peer[0], device_id_type=MESH).wait_recv()

    gathers = [(copy_to(sgat.at[LAST], sgat, 0, p, ROW_BACK, row_peer),
                copy_to(tgat.at[LAST], tgat, 1, p, COL_BACK, col_peer))[axis] for _, axis, p in far]
    for copy in gathers:
        copy.start()
    source_returns = [copy_to(ps.at[p], qs, 2, p, ROW_BACK, row_peer) for p in range(LAST)]
    target_returns = [copy_to(pt.at[p], qt, 3, p, COL_BACK, col_peer) for p in range(LAST)]

    zeros = jnp.zeros((OWN - 48, OWN), f32)

    def prepare_source(d):
        tile = sgat[d]
        at = pl.ds(pl.multiple_of(d * OWN, OWN), OWN)
        rc[:, at], rg[:, at] = moments(tile)
        x, v = tile[0:3], tile[3:6]
        vec = jnp.concatenate([-3.0 * v, -3.0 * x, 3.0 * jnp.sum(x * v, axis=0, keepdims=True), tile[6:7]], axis=0)
        h, m, l = pieces(vec)
        fs[:, at] = jnp.concatenate([h, m, h, m, l, h, zeros], axis=0).astype(bf16)
        xs[:, at] = tile

    def prepare_target(d):
        tile = tgat[d]
        at = pl.ds(pl.multiple_of(d * OWN, OWN), OWN)
        tc[:, at], tg[:, at] = moments(tile)
        x, v = tile[0:3], tile[3:6]
        vec = jnp.concatenate([x, v, tile[6:7], 3.0 * jnp.sum(x * v, axis=0, keepdims=True)], axis=0)
        h, m, l = pieces(vec)
        ft[at, :] = jnp.concatenate([h, h, m, m, h, l, zeros], axis=0).T.astype(bf16)
        for c in range(3):
            xb[at, c * OWN:(c + 1) * OWN] = jnp.broadcast_to(tile[c:c + 1], (OWN, OWN)).T

    def arrive_targets(n, _):
        for u in range(4):
            @pl.when(n * 4 + u < LAST)
            def _():
                arrived(tgat.at[LAST], tgat, 1, n * 4 + u, col_peer)
        for u in range(4):
            prepare_target(n * 4 + u)
        return 0

    lax.fori_loop(0, 4, arrive_targets, 0)

    def fold(total):
        return total[0:8] + total[8:16] + total[16:24]

    tiles = tsum.shape[1] // BI

    def features(k):
        rck, rgk = rc[:, k], rg[:, k]
        return jnp.concatenate([rck, rck, rgk, rgk], axis=1)

    def strips(n, _):
        for u in range(SLOTS):
            p = n * SLOTS + u

            @pl.when(p < LAST)
            def _():
                arrived(sgat.at[LAST], sgat, 0, p, row_peer)
        for u in range(SLOTS):
            prepare_source(n * SLOTS + u)
        spans = [pl.ds(pl.multiple_of((n * WIDE + w) * BK, BK), BK) for w in range(WIDE)]
        pulls = [jnp.zeros((32, BK), f32)] * WIDE
        order = [(w, t) for w in range(WIDE) for t in range(tiles)]
        for m in range(len(order) + 1):
            if m < len(order):
                w, t = order[m]
                k, i = spans[w], slice(t * BI, (t + 1) * BI)
                dw = dot(ft[i, :], fs[:, k], 1, 0)
                s = SOFTEN
                for c in range(3):
                    left = xb[i, c * OWN:(c + 1) * OWN]
                    d = xs[c:c + 1, k] - jnp.concatenate([left] * (BK // OWN), axis=1)
                    s = d * d + s
                q = lax.rsqrt(s)
                q2 = q * q
                c = q * q2
                g = (dw * q2) * c
                for x, part in enumerate(halves(c) + halves(g)):
                    pair[m % 2, x] = part
                for x in range(4):
                    turned[m % 2, x] = pair[m % 2, x].T
            if m > 0:
                w, t = order[m - 1]
                k, i = spans[w], slice(t * BI, (t + 1) * BI)
                tci, tgi = tc[:, i], tg[:, i]
                here = [pair[(m - 1) % 2, x] for x in range(4)]
                across = [turned[(m - 1) % 2, x] for x in range(4)]
                pulls[w] = pulls[w] + dot(jnp.concatenate([tci, tci, tgi, tgi], axis=1),
                                          jnp.concatenate(here, axis=0), 1, 0)
                tsum[:, i] += dot(features(k), jnp.concatenate(across, axis=0), 1, 0)
        for w in range(WIDE):
            folded = fold(pulls[w])
            for u in range(BK // OWN):
                ps[n * SLOTS + w * (BK // OWN) + u] = folded[:, u * OWN:(u + 1) * OWN]
        for m in range(LAST // SLOTS + 1):
            @pl.when(n == m)
            def _():
                for copy in source_returns[SLOTS * m:SLOTS * m + SLOTS]:
                    copy.start()
        return 0

    lax.fori_loop(0, xs.shape[1] // (WIDE * BK), strips, 0)
    for p in sorted(range(LAST + 1), key=lambda p: -col_hops(COL_SLOTS[p])):
        pt[p] = fold(tsum[:, p * OWN:(p + 1) * OWN])
        if p < LAST:
            target_returns[p].start()
    for copy in gathers + source_returns:
        copy.wait_send()

    for p in range(LAST):
        arrived(ps.at[0], qs, 2, p, row_peer)
    pull_ref[...] = jnp.concatenate(resolve(sum((qs[p] for p in range(LAST)), ps[LAST]), sgat[LAST]), axis=0)

    for copy in target_returns:
        copy.wait_send()
    for p in range(LAST):
        arrived(pt.at[0], qt, 3, p, col_peer)
    a1, j1 = resolve(sum((qt[p] for p in range(LAST)), pt[LAST]), tgat[LAST])
    x, v, a, j = ts_ref[0:3], ts_ref[3:6], ts_ref[6:9], ts_ref[9:12]
    v1 = v + 0.5 * STEP * (a + a1) + STEP * STEP / 12.0 * (j - j1)
    x1 = x + 0.5 * STEP * (v + v1) + STEP * STEP / 12.0 * (a - a1)
    next_ref[...] = jnp.concatenate([x1, v1, a1, j1], axis=0)


def solution(mesh):
    n = (LAST + 1) * OWN
    vmem, hbm = pl.BlockSpec(memory_space=pltpu.VMEM), pl.BlockSpec(memory_space=pltpu.HBM)
    slots = pltpu.VMEM((LAST + 1, 8, OWN), f32)
    call = pl.pallas_call(
        kernel,
        out_shape=(jax.ShapeDtypeStruct((12, OWN), f32), jax.ShapeDtypeStruct((6, OWN), f32)),
        in_specs=[hbm] * 4,
        out_specs=(vmem, vmem),
        scratch_shapes=[
            pltpu.VMEM((12, OWN), f32),
            pltpu.VMEM((1, OWN), f32),
            pltpu.VMEM((12, OWN), f32),
            pltpu.VMEM((1, OWN), f32),
            slots,
            slots,
            pltpu.VMEM((n, OWN), bf16),
            pltpu.VMEM((OWN, n), bf16),
            *[pltpu.VMEM((32, n), bf16)] * 4,
            pltpu.VMEM((n, 3 * OWN), f32),
            pltpu.VMEM((8, n), f32),
            pltpu.VMEM((32, n), f32),
            *[slots] * 4,
            pltpu.VMEM((2, 4, BI, BK), bf16),
            pltpu.VMEM((2, 4, BK, BI), bf16),
            pltpu.SemaphoreType.DMA((4, LAST)),
            pltpu.SemaphoreType.DMA((4, LAST)),
            pltpu.SemaphoreType.DMA((4,)),
        ],
        compiler_params=pltpu.CompilerParams(
            collective_id=0, has_side_effects=True, vmem_limit_bytes=48 << 20),
    )

    def shards(target_state, target_mass, source_state, source_mass):
        return call(*(pltpu.with_memory_space_constraint(x, pltpu.HBM) for x in (target_state, target_mass.reshape(1, OWN), source_state, source_mass.reshape(1, OWN))))

    spec = P(None, ("row", "col"))
    line = P(("row", "col"))
    return jax.shard_map(shards, mesh=mesh, in_specs=(spec, line, spec, line),
                         out_specs=(spec, spec), check_vma=False)
```

```python
import jax
import jax.numpy as jnp
import numpy as np
from jax import lax
from jax.experimental import pallas as pl
from jax.experimental.pallas import tpu as pltpu
from jax.sharding import PartitionSpec as P

STEP = 0.25
SOFTEN = 0.0025
MESH = pl.DeviceIdType.MESH
f32, bf16 = jnp.float32, jnp.bfloat16
OWN = 128


def dot(a, b, ca, cb):
    return lax.dot_general(a, b, (((ca,), (cb,)), ((), ())), preferred_element_type=f32)


def pieces(x):
    high = x.astype(bf16).astype(f32)
    rest = x - high
    mid = rest.astype(bf16).astype(f32)
    return high, mid, (rest - mid).astype(bf16).astype(f32)


def halves(x):
    high = x.astype(bf16)
    return high, (x - high.astype(f32)).astype(bf16)


def predict(state, mass):
    x, v, a, j = state[0:3], state[3:6], state[6:9], state[9:12]
    xp = x + STEP * (v + STEP * (0.5 * a + STEP / 6.0 * j))
    vp = v + STEP * (a + 0.5 * STEP * j)
    return jnp.concatenate([xp, vp, jnp.ones_like(mass), mass], axis=0)


def moments(tile):
    row = lax.broadcasted_iota(jnp.int32, tile.shape, 0)
    mass = jnp.broadcast_to(tile[7:8], tile.shape)
    first = jnp.where(row < 7, tile * mass, 0.0)
    moved = pltpu.roll(first, 3, 0)
    second = jnp.where(row == 7, mass, jnp.where((row >= 3) & (row < 6), -moved, 0.0))
    zero = jnp.zeros_like(tile)
    return (
        jnp.concatenate([*pieces(first), zero], axis=0).astype(bf16),
        jnp.concatenate([*pieces(second), zero], axis=0).astype(bf16),
    )


def resolve(total, tile):
    x, v = tile[0:3], tile[3:6]
    accel = total[0:3] - x * total[6:7]
    jerk = total[3:6] - v * total[6:7] + x * total[7:8]
    return accel, jerk


TARGET_SIZES, SOURCE_SIZES = (4, 4), (8, 2)


def target_hops(o):
    return min(o[0], 4 - o[0]) + min(o[1], 4 - o[1])


def source_hops(o):
    return min(o[0], 8 - o[0]) + 0.5 * o[1]


def spread(near):
    return near[7:11] + near[11:][::-1] + near[3:7][::-1] + near[:3][::-1]


def order(sizes, distance, arrange):
    offsets = list(np.ndindex(*sizes))
    return arrange(sorted(offsets[1:], key=distance)) + offsets[:1]


TARGET_SLOTS = order(TARGET_SIZES, target_hops, lambda near: near[::-1])
SOURCE_SLOTS = order(SOURCE_SIZES, source_hops, spread)


def inverse(slots, sizes):
    return [slots.index(tuple(-a % n for a, n in zip(o, sizes))) for o in slots]


TARGET_BACK, SOURCE_BACK = inverse(TARGET_SLOTS, TARGET_SIZES), inverse(SOURCE_SLOTS, SOURCE_SIZES)
LAST = 15
BI = BK = 256
WIDE = 2
SLOTS = WIDE * BK // OWN
GROUP = 8


def peers(row, col):
    z, core, y = lax.rem(row, 8), lax.rem(col, 2), lax.rem(lax.div(col, 2), 4)
    x = lax.div(row, 8) * 2 + lax.div(col, 8)
    plane, line = [], []
    for dx, dy in TARGET_SLOTS:
        to_x, to_y = lax.rem(x + dx, 4), lax.rem(y + dy, 4)
        plane.append((lax.div(to_x, 2) * 8 + z, (lax.rem(to_x, 2) * 4 + to_y) * 2 + core))
    for dz, dc in SOURCE_SLOTS:
        line.append((row - z + lax.rem(z + dz, 8), col - core + lax.rem(core + dc, 2)))
    return plane, line


def kernel(ts_hbm, tm_hbm, ss_hbm, sm_hbm, next_ref, pull_ref, ts_ref, tm_ref, ss_ref, sm_ref,
           tgat, sgat, select, ft, fs, rc, rg, tc, tg, xb, xs, tsum, pt, ps, qt, qs, pair, turned, send, recv, load):
    row, col = lax.axis_index("row"), lax.axis_index("col")
    target_peer, source_peer = peers(row, col)
    far = sorted([(-source_hops(SOURCE_SLOTS[p]), 0, p) for p in range(LAST)]
                 + [(-target_hops(TARGET_SLOTS[p]), 1, p) for p in range(LAST)])

    loads = [pltpu.make_async_copy(a, b, load.at[n]) for n, (a, b) in enumerate(
        ((ts_hbm, ts_ref), (tm_hbm, tm_ref), (ss_hbm, ss_ref), (sm_hbm, sm_ref)))]
    for copy in loads:
        copy.start()
    barrier = pltpu.get_barrier_semaphore()
    for _, axis, p in far:
        pl.semaphore_signal(barrier, inc=1, device_id=(source_peer, target_peer)[axis][p], device_id_type=MESH)
    tsum[...] = jnp.zeros_like(tsum)
    feature = lax.broadcasted_iota(jnp.int32, select.shape, 0)
    axis = lax.broadcasted_iota(jnp.int32, select.shape, 1)
    wanted = (axis >= OWN).astype(jnp.int32) + (axis >= 2 * OWN).astype(jnp.int32)
    chosen = (feature == wanted) | (feature == wanted + 16) | (feature == wanted + 40)
    select[...] = chosen.astype(f32).astype(bf16)
    for copy in loads:
        copy.wait()
    tgat[LAST] = predict(ts_ref[...], tm_ref[...] * (1.0 / 32768))
    sgat[LAST] = predict(ss_ref[...], sm_ref[...] * (1.0 / 32768))
    pl.semaphore_wait(barrier, 2 * LAST)

    def copy_to(src, dst, kind, p, back, peer):
        return pltpu.make_async_remote_copy(
            src_ref=src, dst_ref=dst.at[back[p]], send_sem=send.at[kind, p],
            recv_sem=recv.at[kind, back[p]], device_id=peer[p], device_id_type=MESH)

    def arrived(src, dst, kind, p, peer):
        pltpu.make_async_remote_copy(
            src_ref=src, dst_ref=dst.at[p], send_sem=send.at[kind, 0],
            recv_sem=recv.at[kind, p], device_id=peer[0], device_id_type=MESH).wait_recv()

    gathers = [copy_to(tgat.at[LAST], tgat, 1, p, TARGET_BACK, target_peer) for p in range(LAST)]
    gathers += [copy_to(sgat.at[LAST], sgat, 0, p, SOURCE_BACK, source_peer) for _, axis, p in far if axis == 0]
    for copy in gathers:
        copy.start()
    source_returns = [copy_to(ps.at[p], qs, 2, p, SOURCE_BACK, source_peer) for p in range(LAST)]
    target_returns = [copy_to(pt.at[p], qt, 3, p, TARGET_BACK, target_peer) for p in range(LAST)]

    zeros = jnp.zeros((OWN - 48, OWN), f32)

    def span(d):
        return pl.ds(d * OWN if isinstance(d, int) else pl.multiple_of(d * OWN, OWN), OWN)

    def prepare_source(d):
        tile = sgat[d]
        at = span(d)
        rc[:, at], rg[:, at] = moments(tile)
        x, v = tile[0:3], tile[3:6]
        vec = jnp.concatenate([-3.0 * v, -3.0 * x, 3.0 * jnp.sum(x * v, axis=0, keepdims=True), tile[6:7]], axis=0)
        h, m, l = pieces(vec)
        fs[:, at] = jnp.concatenate([h, m, h, m, l, h, zeros], axis=0).astype(bf16)
        xs[:, at] = tile

    def prepare_target(d):
        tile = tgat[d]
        at = span(d)
        tc[:, at], tg[:, at] = moments(tile)
        x, v = tile[0:3], tile[3:6]
        vec = jnp.concatenate([x, v, tile[6:7], 3.0 * jnp.sum(x * v, axis=0, keepdims=True)], axis=0)
        h, m, l = pieces(vec)
        features = jnp.concatenate([h, h, m, m, h, l, zeros], axis=0).T.astype(bf16)
        ft[at, :] = features
        xb[at, :] = dot(features, select[...], 1, 0)

    def arrive_targets(n, _):
        first = LAST + 1 - GROUP - n * GROUP
        for u in range(GROUP):
            @pl.when(first + u < LAST)
            def _():
                arrived(tgat.at[LAST], tgat, 1, first + u, target_peer)
        for u in range(GROUP):
            prepare_target(first + u)
        return 0

    lax.fori_loop(0, (LAST + 1) // GROUP, arrive_targets, 0)

    def fold(total):
        return total[0:8] + total[8:16] + total[16:24]

    tiles = tsum.shape[1] // BI

    def features(k):
        rck, rgk = rc[:, k], rg[:, k]
        return jnp.concatenate([rck, rck, rgk, rgk], axis=1)

    passes = xs.shape[1] // (WIDE * BK)

    def strips(n, _):
        for u in range(SLOTS):
            p = n * SLOTS + u

            @pl.when(p < LAST)
            def _():
                arrived(sgat.at[LAST], sgat, 0, p, source_peer)
        for u in range(SLOTS):
            prepare_source(n * SLOTS + u)
        spans = [pl.ds(pl.multiple_of((n * WIDE + w) * BK, BK), BK) for w in range(WIDE)]
        order = [(w, t) for w in range(WIDE) for t in range(tiles)]
        pulls = [jnp.zeros((32, BK), f32)] * WIDE
        for m in range(len(order) + 1):
            if m < len(order):
                w, t = order[m]
                k, i = spans[w], slice(t * BI, (t + 1) * BI)
                dw = dot(ft[i, :], fs[:, k], 1, 0)
                s = SOFTEN
                for c in range(3):
                    left = xb[i, c * OWN:(c + 1) * OWN]
                    d = xs[c:c + 1, k] - jnp.concatenate([left] * (BK // OWN), axis=1)
                    s = d * d + s
                q = lax.rsqrt(s)
                q2 = q * q
                c = q * q2
                g = (dw * q2) * c
                for x, part in enumerate(halves(c) + halves(g)):
                    pair[m % 2, x] = part
                for x in range(4):
                    turned[m % 2, x] = pair[m % 2, x].T
            if m > 0:
                w, t = order[m - 1]
                k, i = spans[w], slice(t * BI, (t + 1) * BI)
                tci, tgi = tc[:, i], tg[:, i]
                here = [pair[(m - 1) % 2, x] for x in range(4)]
                across = [turned[(m - 1) % 2, x] for x in range(4)]
                pulls[w] = pulls[w] + dot(jnp.concatenate([tci, tci, tgi, tgi], axis=1),
                                          jnp.concatenate(here, axis=0), 1, 0)
                tsum[:, i] += dot(features(k), jnp.concatenate(across, axis=0), 1, 0)
        for w in range(WIDE):
            folded = fold(pulls[w])
            for u in range(BK // OWN):
                ps[n * SLOTS + w * (BK // OWN) + u] = folded[:, u * OWN:(u + 1) * OWN]
        for m in range(passes - 1):
            @pl.when(n == m)
            def _():
                for copy in source_returns[SLOTS * m:SLOTS * m + SLOTS]:
                    copy.start()
        return 0

    lax.fori_loop(0, passes, strips, 0)
    for p in range(LAST + 1):
        pt[p] = fold(tsum[:, p * OWN:(p + 1) * OWN])
        if p < LAST:
            target_returns[p].start()
    for copy in source_returns[SLOTS * (passes - 1):]:
        copy.start()
    for copy in gathers + source_returns:
        copy.wait_send()

    for p in range(LAST):
        arrived(ps.at[0], qs, 2, p, source_peer)
    pull_ref[...] = jnp.concatenate(resolve(sum((qs[p] for p in range(LAST)), ps[LAST]), sgat[LAST]), axis=0)

    for copy in target_returns:
        copy.wait_send()
    for p in range(LAST):
        arrived(pt.at[0], qt, 3, p, target_peer)
    a1, j1 = resolve(sum((qt[p] for p in range(LAST)), pt[LAST]), tgat[LAST])
    x, v, a, j = ts_ref[0:3], ts_ref[3:6], ts_ref[6:9], ts_ref[9:12]
    v1 = v + 0.5 * STEP * (a + a1) + STEP * STEP / 12.0 * (j - j1)
    x1 = x + 0.5 * STEP * (v + v1) + STEP * STEP / 12.0 * (a - a1)
    next_ref[...] = jnp.concatenate([x1, v1, a1, j1], axis=0)


def solution(mesh):
    n = (LAST + 1) * OWN
    vmem, hbm = pl.BlockSpec(memory_space=pltpu.VMEM), pl.BlockSpec(memory_space=pltpu.HBM)
    slots = pltpu.VMEM((LAST + 1, 8, OWN), f32)
    call = pl.pallas_call(
        kernel,
        out_shape=(jax.ShapeDtypeStruct((12, OWN), f32), jax.ShapeDtypeStruct((6, OWN), f32)),
        in_specs=[hbm] * 4,
        out_specs=(vmem, vmem),
        scratch_shapes=[
            pltpu.VMEM((12, OWN), f32),
            pltpu.VMEM((1, OWN), f32),
            pltpu.VMEM((12, OWN), f32),
            pltpu.VMEM((1, OWN), f32),
            slots,
            slots,
            pltpu.VMEM((OWN, 3 * OWN), bf16),
            pltpu.VMEM((n, OWN), bf16),
            pltpu.VMEM((OWN, n), bf16),
            *[pltpu.VMEM((32, n), bf16)] * 4,
            pltpu.VMEM((n, 3 * OWN), f32),
            pltpu.VMEM((8, n), f32),
            pltpu.VMEM((32, n), f32),
            *[slots] * 4,
            pltpu.VMEM((2, 4, BI, BK), bf16),
            pltpu.VMEM((2, 4, BK, BI), bf16),
            pltpu.SemaphoreType.DMA((4, LAST)),
            pltpu.SemaphoreType.DMA((4, LAST)),
            pltpu.SemaphoreType.DMA((4,)),
        ],
        compiler_params=pltpu.CompilerParams(
            collective_id=0, has_side_effects=True, vmem_limit_bytes=48 << 20),
    )

    def shards(target_state, target_mass, source_state, source_mass):
        return call(*(pltpu.with_memory_space_constraint(x, pltpu.HBM) for x in (target_state, target_mass.reshape(1, OWN), source_state, source_mass.reshape(1, OWN))))

    spec = P(None, ("row", "col"))
    line = P(("row", "col"))
    return jax.shard_map(shards, mesh=mesh, in_specs=(spec, line, spec, line),
                         out_specs=(spec, spec), check_vma=False)
```

```python
import jax
import jax.numpy as jnp
import numpy as np
from jax import lax
from jax.experimental import pallas as pl
from jax.experimental.pallas import tpu as pltpu
from jax.sharding import PartitionSpec as P

STEP = 0.25
SOFTEN = 0.0025
MESH = pl.DeviceIdType.MESH
f32, bf16 = jnp.float32, jnp.bfloat16
OWN = 128


def dot(a, b, ca, cb):
    return lax.dot_general(a, b, (((ca,), (cb,)), ((), ())), preferred_element_type=f32)


def pieces(x):
    high = x.astype(bf16).astype(f32)
    rest = x - high
    mid = rest.astype(bf16).astype(f32)
    return high, mid, (rest - mid).astype(bf16).astype(f32)


def halves(x):
    high = x.astype(bf16)
    return high, (x - high.astype(f32)).astype(bf16)


def predict(state, mass):
    x, v, a, j = state[0:3], state[3:6], state[6:9], state[9:12]
    xp = x + STEP * (v + STEP * (0.5 * a + STEP / 6.0 * j))
    vp = v + STEP * (a + 0.5 * STEP * j)
    return jnp.concatenate([xp, vp, jnp.ones_like(mass), mass], axis=0)


def moments(tile):
    row = lax.broadcasted_iota(jnp.int32, tile.shape, 0)
    mass = jnp.broadcast_to(tile[7:8], tile.shape)
    first = jnp.where(row < 7, tile * mass, 0.0)
    moved = pltpu.roll(first, 3, 0)
    second = jnp.where(row == 7, mass, jnp.where((row >= 3) & (row < 6), -moved, 0.0))
    zero = jnp.zeros_like(tile)
    return (
        jnp.concatenate([*pieces(first), zero], axis=0).astype(bf16),
        jnp.concatenate([*pieces(second), zero], axis=0).astype(bf16),
    )


def resolve(total, tile):
    x, v = tile[0:3], tile[3:6]
    accel = total[0:3] - x * total[6:7]
    jerk = total[3:6] - v * total[6:7] + x * total[7:8]
    return accel, jerk


TARGET_SIZES, SOURCE_SIZES = (4, 4), (8, 2)


def target_hops(o):
    return min(o[0], 4 - o[0]) + min(o[1], 4 - o[1])


def source_hops(o):
    return min(o[0], 8 - o[0]) + 0.5 * o[1]


def spread(near):
    return near[::-1]


def order(sizes, distance, arrange):
    offsets = list(np.ndindex(*sizes))
    return arrange(sorted(offsets[1:], key=distance)) + offsets[:1]


TARGET_SLOTS = order(TARGET_SIZES, target_hops, lambda near: near[::-1])
SOURCE_SLOTS = order(SOURCE_SIZES, source_hops, spread)


def inverse(slots, sizes):
    return [slots.index(tuple(-a % n for a, n in zip(o, sizes))) for o in slots]


TARGET_BACK, SOURCE_BACK = inverse(TARGET_SLOTS, TARGET_SIZES), inverse(SOURCE_SLOTS, SOURCE_SIZES)
LAST = 15
BI = BK = 256
WIDE = 4
SLOTS = WIDE * BK // OWN
GROUP = 8


def peers(row, col):
    z, core, y = lax.rem(row, 8), lax.rem(col, 2), lax.rem(lax.div(col, 2), 4)
    x = lax.div(row, 8) * 2 + lax.div(col, 8)
    plane, line = [], []
    for dx, dy in TARGET_SLOTS:
        to_x, to_y = lax.rem(x + dx, 4), lax.rem(y + dy, 4)
        plane.append((lax.div(to_x, 2) * 8 + z, (lax.rem(to_x, 2) * 4 + to_y) * 2 + core))
    for dz, dc in SOURCE_SLOTS:
        line.append((row - z + lax.rem(z + dz, 8), col - core + lax.rem(core + dc, 2)))
    return plane, line


def kernel(ts_hbm, tm_hbm, ss_hbm, sm_hbm, next_ref, pull_ref, ts_ref, tm_ref, ss_ref, sm_ref,
           tgat, sgat, select, ft, fs, rc, rg, tc, tg, xb, xs, tsum, pt, ps, qt, qs, pair, turned, send, recv, load):
    row, col = lax.axis_index("row"), lax.axis_index("col")
    target_peer, source_peer = peers(row, col)
    far = sorted([(-source_hops(SOURCE_SLOTS[p]), 0, p) for p in range(LAST)]
                 + [(-target_hops(TARGET_SLOTS[p]), 1, p) for p in range(LAST)])

    loads = [pltpu.make_async_copy(a, b, load.at[n]) for n, (a, b) in enumerate(
        ((ts_hbm, ts_ref), (tm_hbm, tm_ref), (ss_hbm, ss_ref), (sm_hbm, sm_ref)))]
    for copy in loads:
        copy.start()
    barrier = pltpu.get_barrier_semaphore()
    for _, axis, p in far:
        pl.semaphore_signal(barrier, inc=1, device_id=(source_peer, target_peer)[axis][p], device_id_type=MESH)
    tsum[...] = jnp.zeros_like(tsum)
    feature = lax.broadcasted_iota(jnp.int32, select.shape, 0)
    axis = lax.broadcasted_iota(jnp.int32, select.shape, 1)
    wanted = (axis >= OWN).astype(jnp.int32) + (axis >= 2 * OWN).astype(jnp.int32)
    chosen = (feature == wanted) | (feature == wanted + 16) | (feature == wanted + 40)
    select[...] = chosen.astype(f32).astype(bf16)
    for copy in loads:
        copy.wait()
    tgat[LAST] = predict(ts_ref[...], tm_ref[...] * (1.0 / 32768))
    sgat[LAST] = predict(ss_ref[...], sm_ref[...] * (1.0 / 32768))
    pl.semaphore_wait(barrier, 2 * LAST)

    def copy_to(src, dst, kind, p, back, peer):
        return pltpu.make_async_remote_copy(
            src_ref=src, dst_ref=dst.at[back[p]], send_sem=send.at[kind, p],
            recv_sem=recv.at[kind, back[p]], device_id=peer[p], device_id_type=MESH)

    def arrived(src, dst, kind, p, peer):
        pltpu.make_async_remote_copy(
            src_ref=src, dst_ref=dst.at[p], send_sem=send.at[kind, 0],
            recv_sem=recv.at[kind, p], device_id=peer[0], device_id_type=MESH).wait_recv()

    gathers = [copy_to(tgat.at[LAST], tgat, 1, p, TARGET_BACK, target_peer) for p in range(LAST)]
    gathers += [copy_to(sgat.at[LAST], sgat, 0, p, SOURCE_BACK, source_peer) for _, axis, p in far if axis == 0]
    for copy in gathers:
        copy.start()
    source_returns = [copy_to(ps.at[p], qs, 2, p, SOURCE_BACK, source_peer) for p in range(LAST)]
    target_returns = [copy_to(pt.at[p], qt, 3, p, TARGET_BACK, target_peer) for p in range(LAST)]

    zeros = jnp.zeros((OWN - 48, OWN), f32)

    def span(d):
        return pl.ds(d * OWN if isinstance(d, int) else pl.multiple_of(d * OWN, OWN), OWN)

    def prepare_source(d):
        tile = sgat[d]
        at = span(d)
        rc[:, at], rg[:, at] = moments(tile)
        x, v = tile[0:3], tile[3:6]
        vec = jnp.concatenate([-3.0 * v, -3.0 * x, 3.0 * jnp.sum(x * v, axis=0, keepdims=True), tile[6:7]], axis=0)
        h, m, l = pieces(vec)
        fs[:, at] = jnp.concatenate([h, m, h, m, l, h, zeros], axis=0).astype(bf16)
        xs[:, at] = tile

    def prepare_target(d):
        tile = tgat[d]
        at = span(d)
        tc[:, at], tg[:, at] = moments(tile)
        x, v = tile[0:3], tile[3:6]
        vec = jnp.concatenate([x, v, tile[6:7], 3.0 * jnp.sum(x * v, axis=0, keepdims=True)], axis=0)
        h, m, l = pieces(vec)
        features = jnp.concatenate([h, h, m, m, h, l, zeros], axis=0).T.astype(bf16)
        ft[at, :] = features
        xb[at, :] = dot(features, select[...], 1, 0)

    def arrive_targets(n, _):
        first = LAST + 1 - GROUP - n * GROUP
        for u in range(GROUP):
            @pl.when(first + u < LAST)
            def _():
                arrived(tgat.at[LAST], tgat, 1, first + u, target_peer)
        for u in range(GROUP):
            prepare_target(first + u)
        return 0

    lax.fori_loop(0, (LAST + 1) // GROUP, arrive_targets, 0)

    def fold(total):
        return total[0:8] + total[8:16] + total[16:24]

    tiles = tsum.shape[1] // BI

    def features(k):
        rck, rgk = rc[:, k], rg[:, k]
        return jnp.concatenate([rck, rck, rgk, rgk], axis=1)

    passes = xs.shape[1] // (WIDE * BK)

    def strips(n, _):
        for u in range(SLOTS):
            p = n * SLOTS + u

            @pl.when(p < LAST)
            def _():
                arrived(sgat.at[LAST], sgat, 0, p, source_peer)
        for u in range(SLOTS):
            prepare_source(n * SLOTS + u)
        spans = [pl.ds(pl.multiple_of((n * WIDE + w) * BK, BK), BK) for w in range(WIDE)]
        order = [(w, t) for w in range(WIDE) for t in range(tiles)]
        pulls = [jnp.zeros((8, BK), f32)] * WIDE
        for m in range(len(order) + 1):
            if m < len(order):
                w, t = order[m]
                k, i = spans[w], slice(t * BI, (t + 1) * BI)
                dw = dot(ft[i, :], fs[:, k], 1, 0)
                s = SOFTEN
                for c in range(3):
                    left = xb[i, c * OWN:(c + 1) * OWN]
                    d = xs[c:c + 1, k] - jnp.concatenate([left] * (BK // OWN), axis=1)
                    s = d * d + s
                q = lax.rsqrt(s)
                q2 = q * q
                c = q * q2
                g = (dw * q2) * c
                for x, part in enumerate(halves(c) + halves(g)):
                    pair[m % 2, x] = part
                for x in range(4):
                    turned[m % 2, x] = pair[m % 2, x].T
            if m > 0:
                w, t = order[m - 1]
                k, i = spans[w], slice(t * BI, (t + 1) * BI)
                tci, tgi = tc[:, i], tg[:, i]
                here = [pair[(m - 1) % 2, x] for x in range(4)]
                across = [turned[(m - 1) % 2, x] for x in range(4)]
                pulls[w] = pulls[w] + fold(dot(jnp.concatenate([tci, tci, tgi, tgi], axis=1),
                                          jnp.concatenate(here, axis=0), 1, 0))
                tsum[:, i] += fold(dot(features(k), jnp.concatenate(across, axis=0), 1, 0))
        for w in range(WIDE):
            folded = pulls[w]
            for u in range(BK // OWN):
                ps[n * SLOTS + w * (BK // OWN) + u] = folded[:, u * OWN:(u + 1) * OWN]
        for m in range(passes - 1):
            @pl.when(n == m)
            def _():
                for copy in source_returns[SLOTS * m:SLOTS * m + SLOTS]:
                    copy.start()
        return 0

    lax.fori_loop(0, passes, strips, 0)
    for p in range(LAST + 1):
        pt[p] = tsum[:, p * OWN:(p + 1) * OWN]
        if p < LAST:
            target_returns[p].start()
    for copy in source_returns[SLOTS * (passes - 1):]:
        copy.start()
    for copy in gathers + source_returns:
        copy.wait_send()

    for p in range(LAST):
        arrived(ps.at[0], qs, 2, p, source_peer)
    pull_ref[...] = jnp.concatenate(resolve(sum((qs[p] for p in range(LAST)), ps[LAST]), sgat[LAST]), axis=0)

    for copy in target_returns:
        copy.wait_send()
    for p in range(LAST):
        arrived(pt.at[0], qt, 3, p, target_peer)
    a1, j1 = resolve(sum((qt[p] for p in range(LAST)), pt[LAST]), tgat[LAST])
    x, v, a, j = ts_ref[0:3], ts_ref[3:6], ts_ref[6:9], ts_ref[9:12]
    v1 = v + 0.5 * STEP * (a + a1) + STEP * STEP / 12.0 * (j - j1)
    x1 = x + 0.5 * STEP * (v + v1) + STEP * STEP / 12.0 * (a - a1)
    next_ref[...] = jnp.concatenate([x1, v1, a1, j1], axis=0)


def solution(mesh):
    n = (LAST + 1) * OWN
    vmem, hbm = pl.BlockSpec(memory_space=pltpu.VMEM), pl.BlockSpec(memory_space=pltpu.HBM)
    slots = pltpu.VMEM((LAST + 1, 8, OWN), f32)
    call = pl.pallas_call(
        kernel,
        out_shape=(jax.ShapeDtypeStruct((12, OWN), f32), jax.ShapeDtypeStruct((6, OWN), f32)),
        in_specs=[hbm] * 4,
        out_specs=(vmem, vmem),
        scratch_shapes=[
            pltpu.VMEM((12, OWN), f32),
            pltpu.VMEM((1, OWN), f32),
            pltpu.VMEM((12, OWN), f32),
            pltpu.VMEM((1, OWN), f32),
            slots,
            slots,
            pltpu.VMEM((OWN, 3 * OWN), bf16),
            pltpu.VMEM((n, OWN), bf16),
            pltpu.VMEM((OWN, n), bf16),
            *[pltpu.VMEM((32, n), bf16)] * 4,
            pltpu.VMEM((n, 3 * OWN), f32),
            pltpu.VMEM((8, n), f32),
            pltpu.VMEM((8, n), f32),
            *[slots] * 4,
            pltpu.VMEM((2, 4, BI, BK), bf16),
            pltpu.VMEM((2, 4, BK, BI), bf16),
            pltpu.SemaphoreType.DMA((4, LAST)),
            pltpu.SemaphoreType.DMA((4, LAST)),
            pltpu.SemaphoreType.DMA((4,)),
        ],
        compiler_params=pltpu.CompilerParams(
            collective_id=0, has_side_effects=True, vmem_limit_bytes=48 << 20),
    )

    def shards(target_state, target_mass, source_state, source_mass):
        return call(*(pltpu.with_memory_space_constraint(x, pltpu.HBM) for x in (target_state, target_mass.reshape(1, OWN), source_state, source_mass.reshape(1, OWN))))

    spec = P(None, ("row", "col"))
    line = P(("row", "col"))
    return jax.shard_map(shards, mesh=mesh, in_specs=(spec, line, spec, line),
                         out_specs=(spec, spec), check_vma=False)
```

```python
import jax
import jax.numpy as jnp
import numpy as np
from jax import lax
from jax.experimental import pallas as pl
from jax.experimental.pallas import tpu as pltpu
from jax.sharding import PartitionSpec as P

STEP = 0.25
SOFTEN = 0.0025
MESH = pl.DeviceIdType.MESH
f32, bf16 = jnp.float32, jnp.bfloat16
OWN = 128


def dot(a, b, ca, cb):
    return lax.dot_general(a, b, (((ca,), (cb,)), ((), ())), preferred_element_type=f32)


def pieces(x):
    high = x.astype(bf16).astype(f32)
    rest = x - high
    mid = rest.astype(bf16).astype(f32)
    return high, mid, (rest - mid).astype(bf16).astype(f32)


def halves(x):
    high = x.astype(bf16)
    return high, (x - high.astype(f32)).astype(bf16)


def predict(state, mass):
    x, v, a, j = state[0:3], state[3:6], state[6:9], state[9:12]
    xp = x + STEP * (v + STEP * (0.5 * a + STEP / 6.0 * j))
    vp = v + STEP * (a + 0.5 * STEP * j)
    return jnp.concatenate([xp, vp, jnp.ones_like(mass), mass], axis=0)


def moments(tile):
    row = lax.broadcasted_iota(jnp.int32, tile.shape, 0)
    mass = jnp.broadcast_to(tile[7:8], tile.shape)
    first = jnp.where(row < 7, tile * mass, 0.0)
    moved = pltpu.roll(first, 3, 0)
    second = jnp.where(row == 7, mass, jnp.where((row >= 3) & (row < 6), -moved, 0.0))
    zero = jnp.zeros_like(tile)
    return (
        jnp.concatenate([*pieces(first), zero], axis=0).astype(bf16),
        jnp.concatenate([*pieces(second), zero], axis=0).astype(bf16),
    )


def resolve(total, tile):
    x, v = tile[0:3], tile[3:6]
    accel = total[0:3] - x * total[6:7]
    jerk = total[3:6] - v * total[6:7] + x * total[7:8]
    return accel, jerk


TARGET_SIZES, SOURCE_SIZES = (4, 4), (8, 2)


def target_hops(o):
    return min(o[0], 4 - o[0]) + min(o[1], 4 - o[1])


def source_hops(o):
    return min(o[0], 8 - o[0]) + 0.5 * o[1]


def spread(near):
    return near[::-1]


def order(sizes, distance, arrange):
    offsets = list(np.ndindex(*sizes))
    return arrange(sorted(offsets[1:], key=distance)) + offsets[:1]


TARGET_SLOTS = order(TARGET_SIZES, target_hops, lambda near: near[::-1])
SOURCE_SLOTS = order(SOURCE_SIZES, source_hops, spread)


def inverse(slots, sizes):
    return [slots.index(tuple(-a % n for a, n in zip(o, sizes))) for o in slots]


TARGET_BACK, SOURCE_BACK = inverse(TARGET_SLOTS, TARGET_SIZES), inverse(SOURCE_SLOTS, SOURCE_SIZES)
LAST = 15
BI = BK = 256
WIDE = 4
SLOTS = WIDE * BK // OWN
GROUP = 8


def peers(row, col):
    z, core, y = lax.rem(row, 8), lax.rem(col, 2), lax.rem(lax.div(col, 2), 4)
    x = lax.div(row, 8) * 2 + lax.div(col, 8)
    plane, line = [], []
    for dx, dy in TARGET_SLOTS:
        to_x, to_y = lax.rem(x + dx, 4), lax.rem(y + dy, 4)
        plane.append((lax.div(to_x, 2) * 8 + z, (lax.rem(to_x, 2) * 4 + to_y) * 2 + core))
    for dz, dc in SOURCE_SLOTS:
        line.append((row - z + lax.rem(z + dz, 8), col - core + lax.rem(core + dc, 2)))
    return plane, line


def kernel(ts_hbm, tm_hbm, ss_hbm, sm_hbm, next_ref, pull_ref, ts_ref, tm_ref, ss_ref, sm_ref,
           tgat, sgat, select, ft, fs, rc, rg, tc, tg, xb, xs, tsum, pt, ps, qt, qs, pair, turned, send, recv, load):
    row, col = lax.axis_index("row"), lax.axis_index("col")
    target_peer, source_peer = peers(row, col)
    far = sorted([(-source_hops(SOURCE_SLOTS[p]), 0, p) for p in range(LAST)]
                 + [(-target_hops(TARGET_SLOTS[p]), 1, p) for p in range(LAST)])

    loads = [pltpu.make_async_copy(a, b, load.at[n]) for n, (a, b) in enumerate(
        ((ts_hbm, ts_ref), (tm_hbm, tm_ref), (ss_hbm, ss_ref), (sm_hbm, sm_ref)))]
    for copy in loads:
        copy.start()
    barrier = pltpu.get_barrier_semaphore()
    for _, axis, p in far:
        pl.semaphore_signal(barrier, inc=1, device_id=(source_peer, target_peer)[axis][p], device_id_type=MESH)
    tsum[...] = jnp.zeros_like(tsum)
    feature = lax.broadcasted_iota(jnp.int32, select.shape, 0)
    axis = lax.broadcasted_iota(jnp.int32, select.shape, 1)
    wanted = (axis >= OWN).astype(jnp.int32) + (axis >= 2 * OWN).astype(jnp.int32)
    chosen = (feature == wanted) | (feature == wanted + 16) | (feature == wanted + 40)
    select[...] = chosen.astype(f32).astype(bf16)
    for copy in loads:
        copy.wait()
    tgat[LAST] = predict(ts_ref[...], tm_ref[...] * (1.0 / 32768))
    sgat[LAST] = predict(ss_ref[...], sm_ref[...] * (1.0 / 32768))
    pl.semaphore_wait(barrier, 2 * LAST)

    def copy_to(src, dst, kind, p, back, peer):
        return pltpu.make_async_remote_copy(
            src_ref=src, dst_ref=dst.at[back[p]], send_sem=send.at[kind, p],
            recv_sem=recv.at[kind, back[p]], device_id=peer[p], device_id_type=MESH)

    def arrived(src, dst, kind, p, peer):
        pltpu.make_async_remote_copy(
            src_ref=src, dst_ref=dst.at[p], send_sem=send.at[kind, 0],
            recv_sem=recv.at[kind, p], device_id=peer[0], device_id_type=MESH).wait_recv()

    gathers = [copy_to(tgat.at[LAST], tgat, 1, p, TARGET_BACK, target_peer) for p in range(LAST)]
    gathers += [copy_to(sgat.at[LAST], sgat, 0, p, SOURCE_BACK, source_peer) for _, axis, p in far if axis == 0]
    for copy in gathers:
        copy.start()
    source_returns = [copy_to(ps.at[p], qs, 2, p, SOURCE_BACK, source_peer) for p in range(LAST)]
    target_returns = [copy_to(pt.at[p], qt, 3, p, TARGET_BACK, target_peer) for p in range(LAST)]

    zeros, pad = jnp.zeros((16, OWN), f32), jnp.zeros((64, OWN), f32)

    def span(d):
        return pl.ds(d * OWN if isinstance(d, int) else pl.multiple_of(d * OWN, OWN), OWN)

    def prepare_source(d):
        tile = sgat[d]
        at = span(d)
        rc[:, at], rg[:, at] = moments(tile)
        x, v = tile[0:3], tile[3:6]
        vec = jnp.concatenate([-3.0 * v, -3.0 * x, 3.0 * jnp.sum(x * v, axis=0, keepdims=True), tile[6:7]], axis=0)
        h, m, l = pieces(vec)
        fs[:, at] = jnp.concatenate([h, m, h, m, l, h, zeros], axis=0).astype(bf16)
        xs[:, at] = tile

    def prepare_target(d):
        tile = tgat[d]
        at = span(d)
        tc[:, at], tg[:, at] = moments(tile)
        x, v = tile[0:3], tile[3:6]
        vec = jnp.concatenate([x, v, tile[6:7], 3.0 * jnp.sum(x * v, axis=0, keepdims=True)], axis=0)
        h, m, l = pieces(vec)
        features = jnp.concatenate([h, h, m, m, h, l, zeros, pad], axis=0).T.astype(bf16)
        ft[at, :] = features
        xb[at, :] = dot(features, select[...], 1, 0)

    def arrive_targets(n, _):
        first = LAST + 1 - GROUP - n * GROUP
        for u in range(GROUP):
            @pl.when(first + u < LAST)
            def _():
                arrived(tgat.at[LAST], tgat, 1, first + u, target_peer)
        for u in range(GROUP):
            prepare_target(first + u)
        return 0

    lax.fori_loop(0, (LAST + 1) // GROUP, arrive_targets, 0)

    def fold_two(total):
        return total[0:8] + total[8:16]

    def fold(total):
        return total[0:8] + total[8:16] + total[16:24]

    tiles = tsum.shape[1] // BI

    passes = xs.shape[1] // (WIDE * BK)

    def strips(n, _):
        for u in range(SLOTS):
            p = n * SLOTS + u

            @pl.when(p < LAST)
            def _():
                arrived(sgat.at[LAST], sgat, 0, p, source_peer)
        for u in range(SLOTS):
            prepare_source(n * SLOTS + u)
        spans = [pl.ds(pl.multiple_of((n * WIDE + w) * BK, BK), BK) for w in range(WIDE)]
        order = [(w, t) for w in range(WIDE) for t in range(tiles)]
        pulls = [jnp.zeros((8, BK), f32)] * WIDE
        for m in range(len(order) + 1):
            if m < len(order):
                w, t = order[m]
                k, i = spans[w], slice(t * BI, (t + 1) * BI)
                dw = dot(ft[i, 0:64], fs[:, k], 1, 0)
                s = SOFTEN
                for c in range(3):
                    left = xb[i, c * OWN:(c + 1) * OWN]
                    d = xs[c:c + 1, k] - jnp.concatenate([left] * (BK // OWN), axis=1)
                    s = d * d + s
                q = lax.rsqrt(s)
                q2 = q * q
                c = q * q2
                g = (dw * q2) * c
                for x, part in enumerate(halves(c) + halves(g)):
                    pair[m % 2, x] = part
                for x in range(4):
                    turned[m % 2, x] = pair[m % 2, x].T
            if m > 0:
                w, t = order[m - 1]
                k, i = spans[w], slice(t * BI, (t + 1) * BI)
                tci, tgi = tc[:, i], tg[:, i]
                here = [pair[(m - 1) % 2, x] for x in range(4)]
                across = [turned[(m - 1) % 2, x] for x in range(4)]
                rck, rgk = rc[:, k], rg[:, k]
                pulls[w] = (pulls[w] + fold(dot(jnp.concatenate([tci, tgi], axis=1),
                                                jnp.concatenate(here[::2], axis=0), 1, 0))
                            + fold_two(dot(jnp.concatenate([tci[0:16], tgi[0:16]], axis=1),
                                           jnp.concatenate(here[1::2], axis=0), 1, 0)))
                tsum[:, i] += (fold(dot(jnp.concatenate([rck, rgk], axis=1), jnp.concatenate(across[::2], axis=0), 1, 0))
                               + fold_two(dot(jnp.concatenate([rck[0:16], rgk[0:16]], axis=1),
                                              jnp.concatenate(across[1::2], axis=0), 1, 0)))
        for w in range(WIDE):
            folded = pulls[w]
            for u in range(BK // OWN):
                ps[n * SLOTS + w * (BK // OWN) + u] = folded[:, u * OWN:(u + 1) * OWN]
        for m in range(passes - 1):
            @pl.when(n == m)
            def _():
                for copy in source_returns[SLOTS * m:SLOTS * m + SLOTS]:
                    copy.start()
        return 0

    lax.fori_loop(0, passes, strips, 0)
    for p in range(LAST + 1):
        pt[p] = tsum[:, p * OWN:(p + 1) * OWN]
        if p < LAST:
            target_returns[p].start()
    for copy in source_returns[SLOTS * (passes - 1):]:
        copy.start()
    for copy in gathers + source_returns:
        copy.wait_send()

    for p in range(LAST):
        arrived(ps.at[0], qs, 2, p, source_peer)
    pull_ref[...] = jnp.concatenate(resolve(sum((qs[p] for p in range(LAST)), ps[LAST]), sgat[LAST]), axis=0)

    for copy in target_returns:
        copy.wait_send()
    for p in range(LAST):
        arrived(pt.at[0], qt, 3, p, target_peer)
    a1, j1 = resolve(sum((qt[p] for p in range(LAST)), pt[LAST]), tgat[LAST])
    x, v, a, j = ts_ref[0:3], ts_ref[3:6], ts_ref[6:9], ts_ref[9:12]
    v1 = v + 0.5 * STEP * (a + a1) + STEP * STEP / 12.0 * (j - j1)
    x1 = x + 0.5 * STEP * (v + v1) + STEP * STEP / 12.0 * (a - a1)
    next_ref[...] = jnp.concatenate([x1, v1, a1, j1], axis=0)


def solution(mesh):
    n = (LAST + 1) * OWN
    vmem, hbm = pl.BlockSpec(memory_space=pltpu.VMEM), pl.BlockSpec(memory_space=pltpu.HBM)
    slots = pltpu.VMEM((LAST + 1, 8, OWN), f32)
    call = pl.pallas_call(
        kernel,
        out_shape=(jax.ShapeDtypeStruct((12, OWN), f32), jax.ShapeDtypeStruct((6, OWN), f32)),
        in_specs=[hbm] * 4,
        out_specs=(vmem, vmem),
        scratch_shapes=[
            pltpu.VMEM((12, OWN), f32),
            pltpu.VMEM((1, OWN), f32),
            pltpu.VMEM((12, OWN), f32),
            pltpu.VMEM((1, OWN), f32),
            slots,
            slots,
            pltpu.VMEM((OWN, 3 * OWN), bf16),
            pltpu.VMEM((n, OWN), bf16),
            pltpu.VMEM((64, n), bf16),
            *[pltpu.VMEM((32, n), bf16)] * 4,
            pltpu.VMEM((n, 3 * OWN), f32),
            pltpu.VMEM((8, n), f32),
            pltpu.VMEM((8, n), f32),
            *[slots] * 4,
            pltpu.VMEM((2, 4, BI, BK), bf16),
            pltpu.VMEM((2, 4, BK, BI), bf16),
            pltpu.SemaphoreType.DMA((4, LAST)),
            pltpu.SemaphoreType.DMA((4, LAST)),
            pltpu.SemaphoreType.DMA((4,)),
        ],
        compiler_params=pltpu.CompilerParams(
            collective_id=0, has_side_effects=True, vmem_limit_bytes=48 << 20),
    )

    def shards(target_state, target_mass, source_state, source_mass):
        return call(*(pltpu.with_memory_space_constraint(x, pltpu.HBM) for x in (target_state, target_mass.reshape(1, OWN), source_state, source_mass.reshape(1, OWN))))

    spec = P(None, ("row", "col"))
    line = P(("row", "col"))
    return jax.shard_map(shards, mesh=mesh, in_specs=(spec, line, spec, line),
                         out_specs=(spec, spec), check_vma=False)
```

```python
import jax
import jax.numpy as jnp
import numpy as np
from jax import lax
from jax.experimental import pallas as pl
from jax.experimental.pallas import tpu as pltpu
from jax.sharding import PartitionSpec as P

STEP = 0.25
SOFTEN = 0.0025
MESH = pl.DeviceIdType.MESH
f32, bf16 = jnp.float32, jnp.bfloat16
OWN = 128


def dot(a, b, ca, cb):
    return lax.dot_general(a, b, (((ca,), (cb,)), ((), ())), preferred_element_type=f32)


def pieces(x):
    high = x.astype(bf16).astype(f32)
    rest = x - high
    mid = rest.astype(bf16).astype(f32)
    return high, mid, (rest - mid).astype(bf16).astype(f32)


def halves(x):
    high = x.astype(bf16)
    return high, (x - high.astype(f32)).astype(bf16)


def predict(state, mass):
    x, v, a, j = state[0:3], state[3:6], state[6:9], state[9:12]
    xp = x + STEP * (v + STEP * (0.5 * a + STEP / 6.0 * j))
    vp = v + STEP * (a + 0.5 * STEP * j)
    return jnp.concatenate([xp, vp, jnp.ones_like(mass), mass], axis=0)


def moments(tile):
    row = lax.broadcasted_iota(jnp.int32, tile.shape, 0)
    mass = jnp.broadcast_to(tile[7:8], tile.shape)
    first = jnp.where(row < 7, tile * mass, 0.0)
    moved = pltpu.roll(first, 3, 0)
    second = jnp.where(row == 7, mass, jnp.where((row >= 3) & (row < 6), -moved, 0.0))
    zero = jnp.zeros_like(tile)
    return (
        jnp.concatenate([*pieces(first), zero], axis=0).astype(bf16),
        jnp.concatenate([*pieces(second), zero], axis=0).astype(bf16),
    )


def resolve(total, tile):
    x, v = tile[0:3], tile[3:6]
    accel = total[0:3] - x * total[6:7]
    jerk = total[3:6] - v * total[6:7] + x * total[7:8]
    return accel, jerk


TARGET_SIZES, SOURCE_SIZES = (4, 4), (8, 2)


def target_hops(o):
    return min(o[0], 4 - o[0]) + min(o[1], 4 - o[1])


def source_hops(o):
    return min(o[0], 8 - o[0]) + 0.5 * o[1]


def spread(near):
    return near[::-1]


def order(sizes, distance, arrange):
    offsets = list(np.ndindex(*sizes))
    return arrange(sorted(offsets[1:], key=distance)) + offsets[:1]


TARGET_SLOTS = order(TARGET_SIZES, target_hops, lambda near: near[::-1])
SOURCE_SLOTS = order(SOURCE_SIZES, source_hops, spread)


def inverse(slots, sizes):
    return [slots.index(tuple(-a % n for a, n in zip(o, sizes))) for o in slots]


TARGET_BACK, SOURCE_BACK = inverse(TARGET_SLOTS, TARGET_SIZES), inverse(SOURCE_SLOTS, SOURCE_SIZES)
LAST = 15
BI = BK = 256
WIDE = 4
SLOTS = WIDE * BK // OWN
GROUP = 8


def peers(row, col):
    z, core, y = lax.rem(row, 8), lax.rem(col, 2), lax.rem(lax.div(col, 2), 4)
    x = lax.div(row, 8) * 2 + lax.div(col, 8)
    plane, line = [], []
    for dx, dy in TARGET_SLOTS:
        to_x, to_y = lax.rem(x + dx, 4), lax.rem(y + dy, 4)
        plane.append((lax.div(to_x, 2) * 8 + z, (lax.rem(to_x, 2) * 4 + to_y) * 2 + core))
    for dz, dc in SOURCE_SLOTS:
        line.append((row - z + lax.rem(z + dz, 8), col - core + lax.rem(core + dc, 2)))
    return plane, line


def kernel(ts_hbm, tm_hbm, ss_hbm, sm_hbm, next_ref, pull_ref, ts_ref, tm_ref, ss_ref, sm_ref,
           tgat, sgat, select, ft, fs, rc, rg, tc, tg, xb, xs, tsum, pt, ps, qt, qs, pair, turned, send, recv, load):
    row, col = lax.axis_index("row"), lax.axis_index("col")
    target_peer, source_peer = peers(row, col)
    far = sorted([(-source_hops(SOURCE_SLOTS[p]), 0, p) for p in range(LAST)]
                 + [(-target_hops(TARGET_SLOTS[p]), 1, p) for p in range(LAST)])

    loads = [pltpu.make_async_copy(a, b, load.at[n]) for n, (a, b) in enumerate(
        ((ts_hbm, ts_ref), (tm_hbm, tm_ref), (ss_hbm, ss_ref), (sm_hbm, sm_ref)))]
    for copy in loads:
        copy.start()
    barrier = pltpu.get_barrier_semaphore()
    for _, axis, p in far:
        pl.semaphore_signal(barrier, inc=1, device_id=(source_peer, target_peer)[axis][p], device_id_type=MESH)
    tsum[...] = jnp.zeros_like(tsum)
    feature = lax.broadcasted_iota(jnp.int32, select.shape, 0)
    axis = lax.broadcasted_iota(jnp.int32, select.shape, 1)
    wanted = (axis >= OWN).astype(jnp.int32) + (axis >= 2 * OWN).astype(jnp.int32)
    chosen = (feature == wanted) | (feature == wanted + 16) | (feature == wanted + 40)
    select[...] = chosen.astype(f32).astype(bf16)
    for copy in loads:
        copy.wait()
    tgat[LAST] = predict(ts_ref[...], tm_ref[...] * (1.0 / 32768))
    sgat[LAST] = predict(ss_ref[...], sm_ref[...] * (1.0 / 32768))
    pl.semaphore_wait(barrier, 2 * LAST)

    def copy_to(src, dst, kind, p, back, peer):
        return pltpu.make_async_remote_copy(
            src_ref=src, dst_ref=dst.at[back[p]], send_sem=send.at[kind, p],
            recv_sem=recv.at[kind, back[p]], device_id=peer[p], device_id_type=MESH)

    def arrived(src, dst, kind, p, peer):
        pltpu.make_async_remote_copy(
            src_ref=src, dst_ref=dst.at[p], send_sem=send.at[kind, 0],
            recv_sem=recv.at[kind, p], device_id=peer[0], device_id_type=MESH).wait_recv()

    gathers = [copy_to(tgat.at[LAST], tgat, 1, p, TARGET_BACK, target_peer) for p in range(LAST)]
    gathers += [copy_to(sgat.at[LAST], sgat, 0, p, SOURCE_BACK, source_peer) for _, axis, p in far if axis == 0]
    for copy in gathers:
        copy.start()
    source_returns = [copy_to(ps.at[p], qs, 2, p, SOURCE_BACK, source_peer) for p in range(LAST)]
    target_returns = [copy_to(pt.at[p], qt, 3, p, TARGET_BACK, target_peer) for p in range(LAST)]

    zeros = jnp.zeros((OWN - 48, OWN), f32)

    def span(d):
        return pl.ds(d * OWN if isinstance(d, int) else pl.multiple_of(d * OWN, OWN), OWN)

    def prepare_source(d):
        tile = sgat[d]
        at = span(d)
        rc[:, at], rg[:, at] = moments(tile)
        x, v = tile[0:3], tile[3:6]
        vec = jnp.concatenate([-3.0 * v, -3.0 * x, 3.0 * jnp.sum(x * v, axis=0, keepdims=True), tile[6:7]], axis=0)
        h, m, l = pieces(vec)
        fs[:, at] = jnp.concatenate([h, m, h, m, l, h], axis=0).astype(bf16)
        xs[:, at] = tile

    def prepare_target(d):
        tile = tgat[d]
        at = span(d)
        tc[:, at], tg[:, at] = moments(tile)
        x, v = tile[0:3], tile[3:6]
        vec = jnp.concatenate([x, v, tile[6:7], 3.0 * jnp.sum(x * v, axis=0, keepdims=True)], axis=0)
        h, m, l = pieces(vec)
        features = jnp.concatenate([h, h, m, m, h, l, zeros], axis=0).T.astype(bf16)
        ft[at, :] = features
        xb[at, :] = dot(features, select[...], 1, 0)

    def arrive_targets(n, _):
        first = LAST + 1 - GROUP - n * GROUP
        for u in range(GROUP):
            @pl.when(first + u < LAST)
            def _():
                arrived(tgat.at[LAST], tgat, 1, first + u, target_peer)
        for u in range(GROUP):
            prepare_target(first + u)
        return 0

    lax.fori_loop(0, (LAST + 1) // GROUP, arrive_targets, 0)

    def fold_two(total):
        return total[0:8] + total[8:16]

    def fold(total):
        return total[0:8] + total[8:16] + total[16:24]

    tiles = tsum.shape[1] // BI

    passes = xs.shape[1] // (WIDE * BK)

    def strips(n, _):
        for u in range(SLOTS):
            p = n * SLOTS + u

            @pl.when(p < LAST)
            def _():
                arrived(sgat.at[LAST], sgat, 0, p, source_peer)
        for u in range(SLOTS):
            prepare_source(n * SLOTS + u)
        spans = [pl.ds(pl.multiple_of((n * WIDE + w) * BK, BK), BK) for w in range(WIDE)]
        order = [(w, t) for w in range(WIDE) for t in range(tiles)]
        pulls = [jnp.zeros((8, BK), f32)] * WIDE
        for m in range(len(order) + 1):
            if m < len(order):
                w, t = order[m]
                k, i = spans[w], slice(t * BI, (t + 1) * BI)
                dw = dot(ft[i, 0:48], fs[:, k], 1, 0)
                s = SOFTEN
                for c in range(3):
                    left = xb[i, c * OWN:(c + 1) * OWN]
                    d = xs[c:c + 1, k] - jnp.concatenate([left] * (BK // OWN), axis=1)
                    s = d * d + s
                q = lax.rsqrt(s)
                q2 = q * q
                c = q * q2
                g = (dw * q2) * c
                for x, part in enumerate(halves(c) + halves(g)):
                    pair[m % 2, x] = part
                for x in range(4):
                    turned[m % 2, x] = pair[m % 2, x].T
            if m > 0:
                w, t = order[m - 1]
                k, i = spans[w], slice(t * BI, (t + 1) * BI)
                tci, tgi = tc[:, i], tg[:, i]
                here = [pair[(m - 1) % 2, x] for x in range(4)]
                across = [turned[(m - 1) % 2, x] for x in range(4)]
                rck, rgk = rc[:, k], rg[:, k]
                pulls[w] = (pulls[w] + fold(dot(jnp.concatenate([tci, tgi], axis=1),
                                                jnp.concatenate(here[::2], axis=0), 1, 0))
                            + fold_two(dot(jnp.concatenate([tci[0:16], tgi[0:16]], axis=1),
                                           jnp.concatenate(here[1::2], axis=0), 1, 0)))
                tsum[:, i] += (fold(dot(jnp.concatenate([rck, rgk], axis=1), jnp.concatenate(across[::2], axis=0), 1, 0))
                               + fold_two(dot(jnp.concatenate([rck[0:16], rgk[0:16]], axis=1),
                                              jnp.concatenate(across[1::2], axis=0), 1, 0)))
        for w in range(WIDE):
            folded = pulls[w]
            for u in range(BK // OWN):
                ps[n * SLOTS + w * (BK // OWN) + u] = folded[:, u * OWN:(u + 1) * OWN]
        for m in range(passes - 1):
            @pl.when(n == m)
            def _():
                for copy in source_returns[SLOTS * m:SLOTS * m + SLOTS]:
                    copy.start()
        return 0

    lax.fori_loop(0, passes, strips, 0)
    for p in range(LAST + 1):
        pt[p] = tsum[:, p * OWN:(p + 1) * OWN]
        if p < LAST:
            target_returns[p].start()
    for copy in source_returns[SLOTS * (passes - 1):]:
        copy.start()
    for copy in gathers + source_returns:
        copy.wait_send()

    for p in range(LAST):
        arrived(ps.at[0], qs, 2, p, source_peer)
    pull_ref[...] = jnp.concatenate(resolve(sum((qs[p] for p in range(LAST)), ps[LAST]), sgat[LAST]), axis=0)

    for copy in target_returns:
        copy.wait_send()
    for p in range(LAST):
        arrived(pt.at[0], qt, 3, p, target_peer)
    a1, j1 = resolve(sum((qt[p] for p in range(LAST)), pt[LAST]), tgat[LAST])
    x, v, a, j = ts_ref[0:3], ts_ref[3:6], ts_ref[6:9], ts_ref[9:12]
    v1 = v + 0.5 * STEP * (a + a1) + STEP * STEP / 12.0 * (j - j1)
    x1 = x + 0.5 * STEP * (v + v1) + STEP * STEP / 12.0 * (a - a1)
    next_ref[...] = jnp.concatenate([x1, v1, a1, j1], axis=0)


def solution(mesh):
    n = (LAST + 1) * OWN
    vmem, hbm = pl.BlockSpec(memory_space=pltpu.VMEM), pl.BlockSpec(memory_space=pltpu.HBM)
    slots = pltpu.VMEM((LAST + 1, 8, OWN), f32)
    call = pl.pallas_call(
        kernel,
        out_shape=(jax.ShapeDtypeStruct((12, OWN), f32), jax.ShapeDtypeStruct((6, OWN), f32)),
        in_specs=[hbm] * 4,
        out_specs=(vmem, vmem),
        scratch_shapes=[
            pltpu.VMEM((12, OWN), f32),
            pltpu.VMEM((1, OWN), f32),
            pltpu.VMEM((12, OWN), f32),
            pltpu.VMEM((1, OWN), f32),
            slots,
            slots,
            pltpu.VMEM((OWN, 3 * OWN), bf16),
            pltpu.VMEM((n, OWN), bf16),
            pltpu.VMEM((48, n), bf16),
            *[pltpu.VMEM((32, n), bf16)] * 4,
            pltpu.VMEM((n, 3 * OWN), f32),
            pltpu.VMEM((8, n), f32),
            pltpu.VMEM((8, n), f32),
            *[slots] * 4,
            pltpu.VMEM((2, 4, BI, BK), bf16),
            pltpu.VMEM((2, 4, BK, BI), bf16),
            pltpu.SemaphoreType.DMA((4, LAST)),
            pltpu.SemaphoreType.DMA((4, LAST)),
            pltpu.SemaphoreType.DMA((4,)),
        ],
        compiler_params=pltpu.CompilerParams(
            collective_id=0, has_side_effects=True, vmem_limit_bytes=48 << 20),
    )

    def shards(target_state, target_mass, source_state, source_mass):
        return call(*(pltpu.with_memory_space_constraint(x, pltpu.HBM) for x in (target_state, target_mass.reshape(1, OWN), source_state, source_mass.reshape(1, OWN))))

    spec = P(None, ("row", "col"))
    line = P(("row", "col"))
    return jax.shard_map(shards, mesh=mesh, in_specs=(spec, line, spec, line),
                         out_specs=(spec, spec), check_vma=False)
```
